128 devices in a mesh: dom: 128 (over x, z, y, core).
Axes of the slice: x: 4, y: 4, z: 4, core: 2. Of those that a mesh axis runs over, the one named last changes fastest.
Arguments:
- feats: bfloat16 [131072, 512], P('dom'), may hold values from -6 to 6
- stale_feats: bfloat16 [131072, 512], P('dom'), may hold values from -6 to 6
- grad_out: bfloat16 [131072, 512], P('dom'), may hold values from -6 to 6
- stale_bgrad: bfloat16 [131072, 512], P('dom'), may hold values from -6 to 6
- w_self: bfloat16 [512, 512], replicated, may hold values from -0.25 to 0.25
- w_neigh: bfloat16 [512, 512], replicated, may hold values from -0.25 to 0.25
- adj_tiles: bfloat16 [1024, 16, 128, 128], P('dom'), may hold values from -0.1875 to 0.1875
- tile_source_rows: int32 [1024, 16], P('dom'), may hold values from 0 to 23
- tile_cnt: int32 [1024], P('dom'), may hold values from 1 to 16, as said below
- send_idx: int32 [16384, 16], P('dom'), may hold values from 0 to 1023
- send_cnt: int32 [128, 128], P('dom'), may hold values from 1 to 16, as said below
Outputs:
- activated: bfloat16 [131072, 512], P('dom')
- grad_feats: bfloat16 [131072, 512], P('dom')
- next_bgrad: bfloat16 [131072, 512], P('dom')
- grad_w_self: float32 [512, 512], replicated
- grad_w_neigh: float32 [512, 512], replicated
The draws below stay inside these ranges and needn't reach their ends.
Inputs may be any that keep to these rules, and one draw needn't show every extreme that they name: `tile_cnt`: each destination tile uses 1 to 16 slots; some destination tile uses all 16 in every draw. `send_cnt`: each pair of partitions uses 1 to 16 slots; every partition fills all 16 slots to some peer in every draw.
All inputs are finite; a program needn't handle non-finite values.
Results may differ from the reference program's by a relative error of at most 0.0064.
Values may be sent and summed in bfloat16 or wider, within the bound.
No kernel may reach another device: no remote copies, remote signals or barrier semaphores. Data moves between devices by JAX's collectives and lax.ppermute only.
A program may use at most 128 MiB of HBM per device.

```python
import jax
import jax.numpy as jnp
from jax import lax

D = 512
TILE = 128
MAXT = 16
NODES_DEV = 1024
CAP = 16
PEERS = 128
TD = 8
STILES = 24
NODES = 131072
N_DOM = 128


def draw_tile_cnt(key, part):
    key = jax.random.fold_in(key, 11)
    key_level, key_base, key_spot = jax.random.split(key, 3)
    levels = jax.random.randint(key_level, (PEERS, 1), 1, 5)
    base_draw = jax.random.randint(key_base, (PEERS, TD), 0, MAXT)
    counts = (1 + base_draw * levels // 4).reshape(-1)
    spot_index = jax.random.randint(key_spot, (), 0, PEERS * TD)
    return jnp.where(jnp.arange(PEERS * TD) == spot_index, MAXT, counts).astype(jnp.int32)


def draw_send_cnt(key, part):
    key = jax.random.fold_in(key, 23)
    key_level, key_base, key_full, key_column = jax.random.split(key, 4)
    levels = jax.random.randint(key_level, (PEERS, 1), 2, 7)
    base_draw = jax.random.randint(key_base, (PEERS, PEERS), 0, CAP)
    counts = jnp.minimum(CAP, 1 + base_draw * levels // 4)
    columns = jnp.arange(PEERS)[None, :]
    full_column = jax.random.randint(key_full, (PEERS, 1), 0, PEERS)
    counts = jnp.where(columns == full_column, CAP, counts)
    full_target = jax.random.randint(key_column, (), 0, PEERS)
    counts = jnp.where(columns == full_target, CAP, counts)
    return counts.astype(jnp.int32)


def set_ends(values, own_key, least, largest):
    shape = values.shape
    spot = [jax.random.randint(jax.random.fold_in(own_key, axis), (), 0, shape[axis]) for axis in range(len(shape))]
    values = values.at[tuple(spot)].set(least)
    longest = shape.index(max(shape))
    spot[longest] = (spot[longest] + 1) % shape[longest]
    return values.at[tuple(spot)].set(largest)


def block_scale(own_key, dims, pieces, low, top_value):
    gain, own = 1.0, jax.random.fold_in(own_key, 6)
    for position, shards_of in pieces:
        steps = jnp.exp(jax.random.uniform(jax.random.fold_in(own, position), (shards_of,), jnp.float32, low / len(pieces), top_value / len(pieces)))
        gain = gain * jnp.repeat(steps, dims[position] // shards_of).reshape([-1 if axis == position else 1 for axis in range(len(dims))])
    return gain


def noise(key, shape, scale, reach, cuts=(), kind=jnp.bfloat16):
    loudness = block_scale(key, shape, cuts, -0.22, 0.18) if cuts else 1.0
    drawn = jax.random.normal(key, shape, jnp.float32) * scale * loudness
    return jnp.minimum(jnp.maximum(drawn, -reach), reach).astype(kind)


def setup_inputs(seed: int = 0) -> dict:
    streams_of = jax.random.split(jax.random.key(seed), 12)
    return {
        "feats": noise(streams_of[0], (NODES, D), 1.0, 6.0, ((0, 128),)),
        "stale_feats": noise(streams_of[1], (NODES, D), 1.0, 6.0, ((0, 128),)),
        "grad_out": noise(streams_of[2], (NODES, D), 1.0, 6.0, ((0, 128),)),
        "stale_bgrad": noise(streams_of[3], (NODES, D), 1.0, 6.0, ((0, 128),)),
        "w_self": noise(streams_of[4], (D, D), D ** -0.5, 0.25),
        "w_neigh": noise(streams_of[5], (D, D), D ** -0.5, 0.25),
        "adj_tiles": noise(streams_of[6], (N_DOM * TD, MAXT, TILE, TILE), (TILE * MAXT // 2) ** -0.5, 0.1875, ((0, 128),)),
        "tile_source_rows": set_ends(jax.random.randint(streams_of[7], (N_DOM * TD, MAXT), 0, STILES), jax.random.fold_in(streams_of[7], 1), 0, STILES - 1).astype(jnp.int32),
        "tile_cnt": draw_tile_cnt(jax.random.fold_in(streams_of[11], 71), 0),
        "send_idx": set_ends(jax.random.randint(streams_of[9], (N_DOM * PEERS, CAP), 0, NODES_DEV), jax.random.fold_in(streams_of[9], 1), 0, NODES_DEV - 1).astype(jnp.int32),
        "send_cnt": draw_send_cnt(jax.random.fold_in(streams_of[11], 71), 0),
    }


def reference(feats, stale_feats, grad_out, stale_bgrad, w_self, w_neigh, adj_tiles, tile_source_rows, tile_cnt, send_idx, send_cnt):
    stale_parts = stale_feats.reshape(PEERS, NODES_DEV, D)
    feat_parts = feats.reshape(PEERS, NODES_DEV, D)
    grad_parts = grad_out.reshape(PEERS, NODES_DEV, D)
    old_grads = stale_bgrad.reshape(PEERS, NODES_DEV, D)
    adj_parts = adj_tiles.reshape(PEERS, TD, MAXT, TILE, TILE)
    src_parts = tile_source_rows.reshape(PEERS, TD, MAXT)
    cnt_parts = tile_cnt.reshape(PEERS, TD)
    index_parts = send_idx.reshape(PEERS, PEERS, CAP)
    owners = jnp.arange(PEERS, dtype=jnp.int32)[:, None]
    live_all = jnp.arange(CAP, dtype=jnp.int32)[None, None, :] < send_cnt[:, :, None]

    def per_device(carry, target):
        next_total, sum_self, sum_neigh = carry
        rows_here = index_parts[:, target, :]
        live_here = live_all[:, target, :]
        incoming = jnp.where(live_here[:, :, None], stale_parts[owners, rows_here], 0).astype(jnp.bfloat16)
        feats_here = feat_parts[target]
        block_groups = jnp.concatenate([feats_here.reshape(TD, TILE, D), incoming.reshape(-1, TILE, D)], axis=0)
        used_tiles = jnp.arange(MAXT, dtype=jnp.int32)[None, :] < cnt_parts[target][:, None]
        edge_weights = jnp.where(used_tiles[:, :, None, None], adj_parts[target], 0).astype(jnp.bfloat16)
        sources = src_parts[target]
        selected_rows = block_groups[sources]
        summed_values = jnp.einsum('xoyc,xoch->xyh', edge_weights.astype(jnp.float32), selected_rows.astype(jnp.float32))
        aggregated = summed_values.reshape(NODES_DEV, D).astype(jnp.bfloat16)
        preact = jnp.dot(feats_here, w_self, preferred_element_type=jnp.float32) + jnp.dot(aggregated, w_neigh, preferred_element_type=jnp.float32)
        activated, pullback = jax.vjp(jax.nn.gelu, preact)
        grad_pre = pullback(grad_parts[target].astype(jnp.float32))[0].astype(jnp.bfloat16)
        sum_self = sum_self + jnp.dot(feats_here.T, grad_pre, preferred_element_type=jnp.float32)
        sum_neigh = sum_neigh + jnp.dot(aggregated.T, grad_pre, preferred_element_type=jnp.float32)
        grad_self = jnp.dot(grad_pre, w_self.T, preferred_element_type=jnp.float32)
        aggregate_gradient = jnp.dot(grad_pre, w_neigh.T, preferred_element_type=jnp.float32).astype(jnp.bfloat16).reshape(TD, TILE, D)
        contribution = jnp.einsum('uxwf,uwn->uxfn', edge_weights.astype(jnp.float32), aggregate_gradient.astype(jnp.float32))
        onehot = (sources.reshape(-1)[:, None] == jnp.arange(STILES, dtype=jnp.int32)[None, :]).astype(jnp.float32)
        grad_source = jnp.einsum('ns,nbd->sbd', onehot, contribution.reshape(-1, TILE, D), precision=lax.Precision.HIGHEST)
        grad_feats = (grad_self + grad_source[:TD].reshape(NODES_DEV, D) + old_grads[target].astype(jnp.float32)).astype(jnp.bfloat16)
        outgoing = grad_source[TD:].reshape(PEERS, CAP, D).astype(jnp.bfloat16)
        returned = jnp.where(live_here[:, :, None], outgoing.astype(jnp.float32), jnp.float32(0.0))
        next_total = next_total.at[owners, rows_here].add(returned)
        return ((next_total, sum_self, sum_neigh), (activated.astype(jnp.bfloat16), grad_feats))
    start = (jnp.zeros((PEERS, NODES_DEV, D), jnp.float32), jnp.zeros((D, D), jnp.float32), jnp.zeros((D, D), jnp.float32))
    (next_total, sum_self, sum_neigh), (activated, grad_feats) = lax.scan(per_device, start, jnp.arange(PEERS, dtype=jnp.int32))
    return (activated.reshape(-1, D), grad_feats.reshape(-1, D), next_total.reshape(-1, D).astype(jnp.bfloat16), sum_self, sum_neigh)
```

```python
import functools

import jax
import jax.numpy as jnp
from jax import lax
from jax.experimental import pallas as pl
from jax.experimental.pallas import tpu as pltpu
from jax.sharding import PartitionSpec as P

BF16 = jnp.bfloat16
F32 = jnp.float32
LANES = 128
MIB = 1 << 20
GELU_SLOPE = 0.7978845608028654
GELU_CUBIC = 0.044715


def dot(a, b):
    return jnp.dot(a, b, preferred_element_type=F32)


def whole(shape):
    return pl.BlockSpec(shape, lambda *_: (0,) * len(shape))


def scalars():
    return pl.BlockSpec(memory_space=pltpu.SMEM)


def params(mib):
    return pltpu.CompilerParams(vmem_limit_bytes=mib * MIB)


def cost(macs, moved):
    return pl.CostEstimate(flops=2 * macs, bytes_accessed=moved, transcendentals=0)


def live_slots(idx_ref, cnt_ref):
    live = lax.broadcasted_iota(jnp.int32, idx_ref.shape, 0) < cnt_ref[...]
    return jnp.where(live, idx_ref[...], -1)


def one_hot(idx, nodes, start, count):
    node_ids = lax.broadcasted_iota(jnp.int32, (idx.shape[0], nodes), 1)
    picks = [
        jnp.where(idx[:, t : t + 1] == node_ids, 1.0, 0.0).astype(BF16)
        for t in range(start, start + count)
    ]
    return jnp.concatenate(picks, axis=0)


def gather_kernel(idx_ref, cnt_ref, rows_ref, out_ref, buf, sems, *, groups):
    slots, peers = idx_ref.shape
    nodes = rows_ref.shape[0]
    idx = live_slots(idx_ref, cnt_ref)
    rows = rows_ref[...]
    per = peers // groups
    copies = []
    for g in range(groups):
        got = dot(one_hot(idx, nodes, g * per, per), rows).astype(BF16)
        span = pl.ds(g * per, per)
        buf[span] = got.reshape(per, slots, rows.shape[1])
        copy = pltpu.make_async_copy(buf.at[span], out_ref.at[span], sems.at[g])
        copy.start()
        copies.append(copy)
    for copy in copies:
        copy.wait()


def gather(slot_rows, send_cnt, stale_feats):
    slots, peers = slot_rows.shape
    nodes, width = stale_feats.shape
    groups = 4
    return pl.pallas_call(
        functools.partial(gather_kernel, groups=groups),
        out_shape=jax.ShapeDtypeStruct((peers, slots, width), BF16),
        in_specs=[pl.BlockSpec(memory_space=pltpu.VMEM)] * 3,
        out_specs=pl.BlockSpec(memory_space=pl.ANY),
        scratch_shapes=[
            pltpu.VMEM((peers, slots, width), BF16),
            pltpu.SemaphoreType.DMA((groups,)),
        ],
        compiler_params=params(24),
        cost_estimate=cost(peers * slots * nodes * width, 3 * MIB),
        name="gather_rows",
    )(slot_rows, send_cnt, stale_feats)


def picks_kernel(idx_ref, cnt_ref, out_ref):
    slots, peers = idx_ref.shape
    nodes = out_ref.shape[0]
    idx = live_slots(idx_ref, cnt_ref)
    per = LANES // slots
    for c in range(peers // per):
        out_ref[:, c * LANES : (c + 1) * LANES] = one_hot(idx, nodes, c * per, per).T


def slot_picks(slot_rows, send_cnt, nodes):
    slots, peers = slot_rows.shape
    return pl.pallas_call(
        picks_kernel,
        out_shape=jax.ShapeDtypeStruct((nodes, peers * slots), BF16),
        in_specs=[pl.BlockSpec(memory_space=pltpu.VMEM)] * 2,
        out_specs=pl.BlockSpec(memory_space=pltpu.VMEM),
        compiler_params=params(16),
        cost_estimate=cost(peers * slots * nodes, 4 * MIB),
        name="slot_picks",
    )(slot_rows, send_cnt)


def combine_kernel(
    src_ref, cnt_ref, adj_ref, feats_ref, ws_ref, wn_ref,
    cb_ref, cbt_ref, cot_ref, self_ref, own_ref, ft_ref, wst_ref, wnt_ref,
    acc,
):
    i = pl.program_id(0)
    tiles, rows = acc.shape[0], acc.shape[1]
    own_tiles = feats_ref.shape[0] // rows
    acc[...] = jnp.zeros_like(acc)

    @pl.when(i == 0)
    def _():
        wst_ref[...] = ws_ref[...].T
        wnt_ref[...] = wn_ref[...].T

    @pl.loop(0, cnt_ref[i])
    def _(j):
        s = src_ref[i, j]
        acc[s] += adj_ref[0, j].astype(F32)

    own = []
    for s in range(tiles):
        block = acc[s].astype(BF16)
        if s < own_tiles:
            own.append(block)
            cot_ref[s * rows : (s + 1) * rows, :] = block.T
        else:
            b = s - own_tiles
            cb_ref[:, b * rows : (b + 1) * rows] = block
            cbt_ref[b * rows : (b + 1) * rows, :] = block.T
    feats = feats_ref[...]
    own_ref[...] = dot(jnp.concatenate(own, axis=1), feats)
    mine = feats_ref[pl.ds(pl.multiple_of(i * rows, rows), rows), :]
    self_ref[...] = dot(mine, ws_ref[...])
    ft_ref[...] = mine.T


def combine(tile_source_rows, tile_cnt, adj_tiles, feats, w_self, w_neigh, all_tiles):
    dst_tiles, slots, rows, _ = adj_tiles.shape
    nodes, width = feats.shape
    bnd = all_tiles * rows - nodes
    out_shape = [
        jax.ShapeDtypeStruct((nodes, bnd), BF16),
        jax.ShapeDtypeStruct((bnd, nodes), BF16),
        jax.ShapeDtypeStruct((nodes, nodes), BF16),
        jax.ShapeDtypeStruct((nodes, width), F32),
        jax.ShapeDtypeStruct((nodes, width), F32),
        jax.ShapeDtypeStruct((width, nodes), BF16),
        jax.ShapeDtypeStruct((width, width), BF16),
        jax.ShapeDtypeStruct((width, width), BF16),
    ]
    return pl.pallas_call(
        combine_kernel,
        grid=(dst_tiles,),
        out_shape=out_shape,
        in_specs=[
            scalars(),
            scalars(),
            pl.BlockSpec((1, slots, rows, rows), lambda i: (i, 0, 0, 0)),
            whole((nodes, width)),
            whole((width, width)),
            whole((width, width)),
        ],
        out_specs=[
            pl.BlockSpec((rows, bnd), lambda i: (i, 0)),
            pl.BlockSpec((bnd, rows), lambda i: (0, i)),
            pl.BlockSpec((nodes, rows), lambda i: (0, i)),
            pl.BlockSpec((rows, width), lambda i: (i, 0)),
            pl.BlockSpec((rows, width), lambda i: (i, 0)),
            pl.BlockSpec((width, rows), lambda i: (0, i)),
            whole((width, width)),
            whole((width, width)),
        ],
        scratch_shapes=[pltpu.VMEM((all_tiles, rows, rows), F32)],
        compiler_params=params(24),
        cost_estimate=cost(nodes * width * (nodes + width), 20 * MIB),
        name="combine_tiles",
    )(tile_source_rows, tile_cnt, adj_tiles, feats, w_self, w_neigh)


def layer_kernel(
    core_ref, cb_ref, in_ref, self_ref, own_ref, gout_ref, wn_ref, wnt_ref, ft_ref,
    act_ref, gpre_ref, gagg_ref, keep_ref, pass_ref,
    gpre_all, aggt_all,
):
    i = pl.program_id(0)
    block = cb_ref.shape[0]
    agg = (own_ref[...] + dot(cb_ref[...], in_ref[...])).astype(BF16)
    pre = self_ref[...] + dot(agg, wn_ref[...])
    square = pre * pre
    t = jnp.tanh(GELU_SLOPE * pre * (1.0 + GELU_CUBIC * square))
    half = 0.5 * (1.0 + t)
    act_ref[...] = (pre * half).astype(BF16)
    slope = half + 0.5 * pre * (1.0 - t * t) * (
        GELU_SLOPE * (1.0 + (3.0 * GELU_CUBIC) * square)
    )
    gpre = (gout_ref[...].astype(F32) * slope).astype(BF16)
    gpre_ref[...] = gpre
    gagg_ref[...] = dot(gpre, wnt_ref[...]).astype(BF16)
    span = pl.ds(pl.multiple_of(i * block, block), block)
    gpre_all[span, :] = gpre
    aggt_all[:, span] = agg.T

    @pl.when(i == pl.num_programs(0) - 1)
    def _():
        first = core_ref[0] == 0
        gp = gpre_all[...]
        width = gp.shape[1]
        groups, halves, rows, lanes = keep_ref.shape
        for part, left in enumerate((ft_ref[...], aggt_all[...])):
            g = dot(left, gp).reshape(groups // 2, rows, width)
            at = pl.ds(part * (groups // 2), groups // 2)
            for h in range(halves):
                even = g[:, :, 2 * h * lanes : (2 * h + 1) * lanes]
                odd = g[:, :, (2 * h + 1) * lanes : (2 * h + 2) * lanes]
                keep_ref[at, h] = jnp.where(first, even, odd)
                pass_ref[at, h] = jnp.where(first, odd, even).astype(BF16)


def layer(core, cb, incoming, self_pre, own_agg, grad_out, w_neigh, w_neigh_t, feats_t, chips):
    nodes, bnd = cb.shape
    width = incoming.shape[1]
    block = 256
    rows = 2 * width // chips
    shares = (chips, width // (2 * LANES), rows, LANES)
    by_block = lambda w: pl.BlockSpec((block, w), lambda i: (i, 0))
    return pl.pallas_call(
        layer_kernel,
        grid=(nodes // block,),
        out_shape=[
            jax.ShapeDtypeStruct((nodes, width), BF16),
            jax.ShapeDtypeStruct((nodes, width), BF16),
            jax.ShapeDtypeStruct((nodes, width), BF16),
            jax.ShapeDtypeStruct(shares, F32),
            jax.ShapeDtypeStruct(shares, BF16),
        ],
        in_specs=[
            scalars(),
            by_block(bnd),
            whole((bnd, width)),
            by_block(width),
            by_block(width),
            by_block(width),
            whole((width, width)),
            whole((width, width)),
            whole((width, nodes)),
        ],
        out_specs=[by_block(width)] * 3 + [whole(shares)] * 2,
        scratch_shapes=[pltpu.VMEM((nodes, width), BF16), pltpu.VMEM((width, nodes), BF16)],
        compiler_params=params(32),
        cost_estimate=cost(nodes * width * (bnd + 4 * width), 16 * MIB),
        name="layer",
    )(core, cb, incoming, self_pre, own_agg, grad_out, w_neigh, w_neigh_t, feats_t)


def boundary_kernel(cbt_ref, gagg_ref, out_ref):
    peers, slots, _ = out_ref.shape
    width = gagg_ref.shape[1]
    got = dot(cbt_ref[...], gagg_ref[...]).astype(BF16)
    out_ref[:, :, :width] = got.reshape(peers, slots, width)


def boundary(cbt, grad_agg, peers, slots):
    bnd, nodes = cbt.shape
    width = grad_agg.shape[1]
    steps = 4
    return pl.pallas_call(
        boundary_kernel,
        grid=(steps,),
        out_shape=jax.ShapeDtypeStruct((peers, slots, width + LANES), BF16),
        in_specs=[
            pl.BlockSpec((bnd // steps, nodes), lambda i: (i, 0)),
            whole((nodes, width)),
        ],
        out_specs=pl.BlockSpec((peers // steps, slots, width + LANES), lambda i: (i, 0, 0)),
        compiler_params=params(24),
        cost_estimate=cost(bnd * nodes * width, 8 * MIB),
        name="boundary_grads",
    )(cbt, grad_agg)


def share_kernel(parts_ref, _, out_ref, buf, sem):
    peers = parts_ref.shape[0]
    for core in range(2):
        total = parts_ref[core].astype(F32)
        for p in range(2 + core, peers, 2):
            total += parts_ref[p].astype(F32)
        total = total.astype(BF16)
        for p in range(core, peers, 2):
            buf[p] = total
    width = out_ref.shape[2] - LANES
    copy = pltpu.make_async_copy(buf, out_ref.at[:, :, pl.ds(width, LANES)], sem)
    copy.start()
    copy.wait()


def lay_shares(parts, rows):
    return pl.pallas_call(
        share_kernel,
        out_shape=jax.ShapeDtypeStruct(rows.shape, BF16),
        in_specs=[pl.BlockSpec(memory_space=pltpu.VMEM), pl.BlockSpec(memory_space=pl.ANY)],
        out_specs=pl.BlockSpec(memory_space=pl.ANY),
        scratch_shapes=[pltpu.VMEM(parts.shape, BF16), pltpu.SemaphoreType.DMA],
        input_output_aliases={1: 0},
        compiler_params=params(16),
        cost_estimate=cost(parts.size, MIB),
        name="lay_shares",
    )(parts, rows)


def feats_grad_kernel(cot_ref, gagg_ref, gpre_ref, wst_ref, stale_ref, out_ref):
    total = dot(gpre_ref[...], wst_ref[...]) + dot(cot_ref[...], gagg_ref[...])
    out_ref[...] = (total + stale_ref[...].astype(F32)).astype(BF16)


def feats_grad(cot, grad_agg, grad_pre, w_self_t, stale_bgrad):
    nodes, width = grad_agg.shape
    block = 256
    by_block = lambda w: pl.BlockSpec((block, w), lambda i: (i, 0))
    return pl.pallas_call(
        feats_grad_kernel,
        grid=(nodes // block,),
        out_shape=jax.ShapeDtypeStruct((nodes, width), BF16),
        in_specs=[
            by_block(nodes),
            whole((nodes, width)),
            by_block(width),
            whole((width, width)),
            by_block(width),
        ],
        out_specs=by_block(width),
        compiler_params=params(24),
        cost_estimate=cost(nodes * width * (nodes + width), 7 * MIB),
        name="feats_grad",
    )(cot, grad_agg, grad_pre, w_self_t, stale_bgrad)


def scatter_kernel(picks_ref, ret_ref, out_ref, buf, sem):
    peers, slots, width = buf.shape
    copy = pltpu.make_async_copy(ret_ref.at[:, :, pl.ds(0, width)], buf, sem)
    copy.start()
    copy.wait()
    out_ref[...] = dot(picks_ref[...], buf[...].reshape(peers * slots, width)).astype(BF16)


def scatter(picks, returned):
    nodes = picks.shape[0]
    peers, slots, padded = returned.shape
    width = padded - LANES
    return pl.pallas_call(
        scatter_kernel,
        out_shape=jax.ShapeDtypeStruct((nodes, width), BF16),
        in_specs=[pl.BlockSpec(memory_space=pltpu.VMEM), pl.BlockSpec(memory_space=pl.ANY)],
        out_specs=pl.BlockSpec(memory_space=pltpu.VMEM),
        scratch_shapes=[pltpu.VMEM((peers, slots, width), BF16), pltpu.SemaphoreType.DMA],
        compiler_params=params(16),
        cost_estimate=cost(peers * slots * nodes * width, 4 * MIB),
        name="scatter_rows",
    )(picks, returned)


def weights_kernel(core_ref, mine_ref, other_ref, ws_ref, wn_ref):
    first = core_ref[0] == 0
    chips, halves, rows, lanes = mine_ref.shape
    for part, out_ref in enumerate((ws_ref, wn_ref)):
        at = pl.ds(part * (chips // 2), chips // 2)
        for h in range(halves):
            mine = mine_ref[at, h].astype(F32).reshape(chips // 2 * rows, lanes)
            other = other_ref[at, h].astype(F32).reshape(chips // 2 * rows, lanes)
            out_ref[:, 2 * h * lanes : (2 * h + 1) * lanes] = jnp.where(first, mine, other)
            out_ref[:, (2 * h + 1) * lanes : (2 * h + 2) * lanes] = jnp.where(first, other, mine)


def lay_weights(core, mine, other, width):
    return pl.pallas_call(
        weights_kernel,
        out_shape=[jax.ShapeDtypeStruct((width, width), F32)] * 2,
        in_specs=[scalars()] + [pl.BlockSpec(memory_space=pltpu.VMEM)] * 2,
        out_specs=[pl.BlockSpec(memory_space=pltpu.VMEM)] * 2,
        compiler_params=params(16),
        cost_estimate=cost(width * width, 3 * MIB),
        name="lay_weights",
    )(core, mine, other)


def body(
    feats,
    stale_feats,
    grad_out,
    stale_bgrad,
    w_self,
    w_neigh,
    adj_tiles,
    tile_source_rows,
    tile_cnt,
    send_idx,
    send_cnt,
):
    peers, slots = send_idx.shape
    nodes, width = feats.shape
    tile_rows = adj_tiles.shape[2]
    all_tiles = (nodes + peers * slots) // tile_rows
    chips = peers // 2
    core = lax.rem(lax.axis_index("dom"), 2).astype(jnp.int32).reshape(1)
    pairs = [(d, d + 1 - 2 * (d % 2)) for d in range(peers)]
    exchange = lambda v: lax.all_to_all(v, "dom", split_axis=0, concat_axis=0, tiled=True)

    slot_rows = send_idx.T
    outgoing = gather(slot_rows, send_cnt, stale_feats)
    incoming = exchange(outgoing).reshape(peers * slots, width)
    cb, cbt, cot, self_pre, own_agg, feats_t, w_self_t, w_neigh_t = combine(
        tile_source_rows, tile_cnt, adj_tiles, feats, w_self, w_neigh, all_tiles
    )
    picks = slot_picks(slot_rows, send_cnt, nodes)

    activated, grad_pre, grad_agg, keep, give = layer(
        core, cb, incoming, self_pre, own_agg, grad_out, w_neigh, w_neigh_t, feats_t, chips
    )
    got = lax.ppermute(give, "dom", pairs)
    pair_sum = (keep + got.astype(F32)).astype(BF16).reshape(peers, -1, LANES)
    parts = exchange(pair_sum)
    rows = boundary(cbt, grad_agg, peers, slots)
    returned = exchange(lay_shares(parts, rows))
    grad_feats = feats_grad(cot, grad_agg, grad_pre, w_self_t, stale_bgrad)

    mine = returned[:, :, width:].reshape(keep.shape)
    other = lax.ppermute(mine, "dom", pairs)
    next_bgrad = scatter(picks, returned)
    grad_w_self, grad_w_neigh = lay_weights(core, mine, other, width)
    return activated, grad_feats, next_bgrad, grad_w_self, grad_w_neigh


def solution(mesh):
    in_specs = (
        P("dom", None),
        P("dom", None),
        P("dom", None),
        P("dom", None),
        P(),
        P(),
        P("dom", None, None, None),
        P("dom", None),
        P("dom"),
        P("dom", None),
        P("dom", None),
    )
    out_specs = (P("dom", None), P("dom", None), P("dom", None), P(), P())
    return jax.shard_map(body, mesh=mesh, in_specs=in_specs, out_specs=out_specs, check_vma=False)
```

```python
import functools

import jax
import jax.numpy as jnp
from jax import lax
from jax.experimental import pallas as pl
from jax.experimental.pallas import tpu as pltpu
from jax.sharding import PartitionSpec as P

BF16 = jnp.bfloat16
F32 = jnp.float32
LANES = 128
MIB = 1 << 20
GELU_SLOPE = 0.7978845608028654
GELU_CUBIC = 0.044715


def dot(a, b):
    return jnp.dot(a, b, preferred_element_type=F32)


def whole(shape):
    return pl.BlockSpec(shape, lambda *_: (0,) * len(shape))


def scalars():
    return pl.BlockSpec(memory_space=pltpu.SMEM)


def anywhere():
    return pl.BlockSpec(memory_space=pl.ANY)


def in_vmem():
    return pl.BlockSpec(memory_space=pltpu.VMEM)


SMALL_PARAMS = pltpu.CompilerParams(vmem_limit_bytes=16 * MIB)
PARAMS = pltpu.CompilerParams(vmem_limit_bytes=56 * MIB)


def cost(macs, moved):
    return pl.CostEstimate(flops=2 * macs, bytes_accessed=moved, transcendentals=0)


def live_slots(idx_ref, cnt_ref):
    live = lax.broadcasted_iota(jnp.int32, idx_ref.shape, 0) < cnt_ref[...]
    return jnp.where(live, idx_ref[...], -1)


def one_hot(idx, nodes, start, count):
    node_ids = lax.broadcasted_iota(jnp.int32, (idx.shape[0], nodes), 1)
    picks = [
        jnp.where(idx[:, t : t + 1] == node_ids, 1.0, 0.0).astype(BF16)
        for t in range(start, start + count)
    ]
    return jnp.concatenate(picks, axis=0)


def gather_kernel(idx_ref, cnt_ref, rows_ref, out_ref, rows, buf, sem, sems, *, groups):
    slots, peers = idx_ref.shape
    nodes, width = rows.shape
    load = pltpu.make_async_copy(rows_ref, rows, sem)
    load.start()
    idx = live_slots(idx_ref, cnt_ref)
    per = peers // groups
    copies = []
    for g in range(groups):
        picks = one_hot(idx, nodes, g * per, per)
        if g == 0:
            load.wait()
        span = pl.ds(g * per, per)
        buf[span] = dot(picks, rows[...]).astype(BF16).reshape(per, slots, width)
        copy = pltpu.make_async_copy(buf.at[span], out_ref.at[span], sems.at[g])
        copy.start()
        copies.append(copy)
    for copy in copies:
        copy.wait()


def gather(slot_rows, send_cnt, stale_feats, groups=8):
    slots, peers = slot_rows.shape
    nodes, width = stale_feats.shape
    return pl.pallas_call(
        functools.partial(gather_kernel, groups=groups),
        out_shape=jax.ShapeDtypeStruct((peers, slots, width), BF16),
        in_specs=[in_vmem()] * 2 + [anywhere()],
        out_specs=anywhere(),
        scratch_shapes=[
            pltpu.VMEM((nodes, width), BF16),
            pltpu.VMEM((peers, slots, width), BF16),
            pltpu.SemaphoreType.DMA,
            pltpu.SemaphoreType.DMA((groups,)),
        ],
        compiler_params=PARAMS,
        cost_estimate=cost(peers * slots * nodes * width, 3 * MIB),
        name="gather_rows",
    )(slot_rows, send_cnt, stale_feats)


def combine_kernel(
    src_ref, cnt_ref, adj_ref, feats_ref, ws_ref, wn_ref,
    cb_ref, cbt_ref, cot_ref, self_ref, own_ref, ft_ref, wst_ref, wnt_ref,
    acc,
):
    i = pl.program_id(0)
    tiles, rows = acc.shape[0], acc.shape[1]
    own_tiles = feats_ref.shape[0] // rows
    acc[...] = jnp.zeros_like(acc)

    @pl.when(i == 0)
    def _():
        wst_ref[...] = ws_ref[...].T
        wnt_ref[...] = wn_ref[...].T

    @pl.loop(0, cnt_ref[i])
    def _(j):
        s = src_ref[i, j]
        acc[s] += adj_ref[0, j].astype(F32)

    own = []
    for s in range(tiles):
        block = acc[s].astype(BF16)
        if s < own_tiles:
            own.append(block)
            cot_ref[s * rows : (s + 1) * rows, :] = block.T
        else:
            b = s - own_tiles
            cb_ref[:, b * rows : (b + 1) * rows] = block
            cbt_ref[b * rows : (b + 1) * rows, :] = block.T
    feats = feats_ref[...]
    own_ref[...] = dot(jnp.concatenate(own, axis=1), feats)
    mine = feats_ref[pl.ds(pl.multiple_of(i * rows, rows), rows), :]
    self_ref[...] = dot(mine, ws_ref[...])
    ft_ref[...] = mine.T


def combine(tile_source_rows, tile_cnt, adj_tiles, feats, w_self, w_neigh, all_tiles):
    dst_tiles, slots, rows, _ = adj_tiles.shape
    nodes, width = feats.shape
    bnd = all_tiles * rows - nodes
    out_shape = [
        jax.ShapeDtypeStruct((nodes, bnd), BF16),
        jax.ShapeDtypeStruct((bnd, nodes), BF16),
        jax.ShapeDtypeStruct((nodes, nodes), BF16),
        jax.ShapeDtypeStruct((nodes, width), F32),
        jax.ShapeDtypeStruct((nodes, width), F32),
        jax.ShapeDtypeStruct((width, nodes), BF16),
        jax.ShapeDtypeStruct((width, width), BF16),
        jax.ShapeDtypeStruct((width, width), BF16),
    ]
    return pl.pallas_call(
        combine_kernel,
        grid=(dst_tiles,),
        out_shape=out_shape,
        in_specs=[
            scalars(),
            scalars(),
            pl.BlockSpec((1, slots, rows, rows), lambda i: (i, 0, 0, 0)),
            whole((nodes, width)),
            whole((width, width)),
            whole((width, width)),
        ],
        out_specs=[
            pl.BlockSpec((rows, bnd), lambda i: (i, 0)),
            pl.BlockSpec((bnd, rows), lambda i: (0, i)),
            pl.BlockSpec((nodes, rows), lambda i: (0, i)),
            pl.BlockSpec((rows, width), lambda i: (i, 0)),
            pl.BlockSpec((rows, width), lambda i: (i, 0)),
            pl.BlockSpec((width, rows), lambda i: (0, i)),
            whole((width, width)),
            whole((width, width)),
        ],
        scratch_shapes=[pltpu.VMEM((all_tiles, rows, rows), F32)],
        compiler_params=PARAMS,
        cost_estimate=cost(nodes * width * (nodes + width), 20 * MIB),
        name="combine_tiles",
    )(tile_source_rows, tile_cnt, adj_tiles, feats, w_self, w_neigh)


class Stream:
    def __init__(self, copies, ahead):
        self.copies, self.ahead, self.started = copies, ahead, 0
        self.start(ahead)

    def start(self, count):
        while self.started < min(count, len(self.copies)):
            self.copies[self.started].start()
            self.started += 1

    def wait(self, *copies):
        for copy in copies:
            at = [c is copy for c in self.copies].index(True)
            self.start(at + 1 + self.ahead)
            copy.wait()


def layer_kernel(
    core_ref, cb_ref, in_ref, self_ref, own_ref, gout_ref, wn_ref, wnt_ref, ft_ref,
    act_ref, gpre_ref, gagg_ref, keep_ref, pass_ref,
    cb, rows_in, self_pre, own, gout, wn, wnt, left, act, gpre, gagg, keep, give,
    cb_sems, in_sems, sems, out_sems,
):
    chunks = cb_sems.shape[0]
    bnd, width = rows_in.shape
    depth = bnd // chunks
    spans = [pl.ds(k * depth, depth) for k in range(chunks)]
    copy = pltpu.make_async_copy
    get_cb = [copy(cb_ref.at[:, d], cb.at[:, d], cb_sems.at[k]) for k, d in enumerate(spans)]
    get_in = [copy(in_ref.at[d], rows_in.at[d], in_sems.at[k]) for k, d in enumerate(spans)]
    rest = [
        (own_ref, own), (wn_ref, wn), (self_ref, self_pre), (gout_ref, gout), (wnt_ref, wnt),
        (ft_ref, left.at[pl.ds(0, width)]),
    ]
    rest = [copy(src, dst, sems.at[n]) for n, (src, dst) in enumerate(rest)]
    loads = Stream([c for pair in zip(get_cb, get_in) for c in pair] + rest, 6)
    outs = []

    def put(src, dst):
        outs.append(copy(src, dst, out_sems.at[len(outs)]))
        outs[-1].start()

    total = None
    for k in range(chunks):
        loads.wait(get_cb[k], get_in[k])
        term = dot(cb[:, k * depth : (k + 1) * depth], rows_in[k * depth : (k + 1) * depth, :])
        total = term if total is None else total + term
    loads.wait(rest[0])
    agg = (total + own[...]).astype(BF16)
    loads.wait(rest[1], rest[2])
    pre = self_pre[...] + dot(agg, wn[...])
    left[width:, :] = agg.T
    square = pre * pre
    t = jnp.tanh(GELU_SLOPE * pre * (1.0 + GELU_CUBIC * square))
    half = 0.5 * (1.0 + t)
    act[...] = (pre * half).astype(BF16)
    slope = half + 0.5 * pre * (1.0 - t * t) * (
        GELU_SLOPE * (1.0 + (3.0 * GELU_CUBIC) * square)
    )
    loads.wait(rest[3], rest[4])
    gpre[...] = (gout[...].astype(F32) * slope).astype(BF16)
    put(act, act_ref)
    put(gpre, gpre_ref)
    gagg[...] = dot(gpre[...], wnt[...]).astype(BF16)
    put(gagg, gagg_ref)
    loads.wait(rest[5])
    first = core_ref[0] == 0
    groups, halves, rows, lanes = keep.shape
    g = dot(left[...], gpre[...]).reshape(groups, rows, width)
    for h in range(halves):
        even = g[:, :, 2 * h * lanes : (2 * h + 1) * lanes]
        odd = g[:, :, (2 * h + 1) * lanes : (2 * h + 2) * lanes]
        keep[:, h] = jnp.where(first, even, odd)
        give[:, h] = jnp.where(first, odd, even).astype(BF16)
    put(give, pass_ref)
    put(keep, keep_ref)
    for c in outs:
        c.wait()


def layer(core, cb, incoming, self_pre, own_agg, grad_out, w_neigh, w_neigh_t, feats_t, chips):
    nodes, bnd = cb.shape
    width = incoming.shape[1]
    chunks = 4
    shares = (chips, width // (2 * LANES), 2 * width // chips, LANES)
    vmem = pltpu.VMEM
    sems = pltpu.SemaphoreType.DMA
    return pl.pallas_call(
        layer_kernel,
        out_shape=[
            jax.ShapeDtypeStruct((nodes, width), BF16),
            jax.ShapeDtypeStruct((nodes, width), BF16),
            jax.ShapeDtypeStruct((nodes, width), BF16),
            jax.ShapeDtypeStruct(shares, F32),
            jax.ShapeDtypeStruct(shares, BF16),
        ],
        in_specs=[scalars()] + [anywhere()] * 8,
        out_specs=[anywhere()] * 5,
        scratch_shapes=[
            vmem((nodes, bnd), BF16),
            vmem((bnd, width), BF16),
            vmem((nodes, width), F32),
            vmem((nodes, width), F32),
            vmem((nodes, width), BF16),
            vmem((width, width), BF16),
            vmem((width, width), BF16),
            vmem((2 * width, nodes), BF16),
            vmem((nodes, width), BF16),
            vmem((nodes, width), BF16),
            vmem((nodes, width), BF16),
            vmem(shares, F32),
            vmem(shares, BF16),
            sems((chunks,)),
            sems((chunks,)),
            sems((6,)),
            sems((5,)),
        ],
        compiler_params=PARAMS,
        cost_estimate=cost(nodes * width * (bnd + 4 * width), 18 * MIB),
        name="layer",
    )(core, cb, incoming, self_pre, own_agg, grad_out, w_neigh, w_neigh_t, feats_t)


def boundary_kernel(cbt_ref, gagg_ref, out_ref):
    peers, slots, _ = out_ref.shape
    width = gagg_ref.shape[1]
    got = dot(cbt_ref[...], gagg_ref[...]).astype(BF16)
    out_ref[:, :, :width] = got.reshape(peers, slots, width)


def boundary(cbt, grad_agg, peers, slots):
    bnd, nodes = cbt.shape
    width = grad_agg.shape[1]
    steps = 4
    return pl.pallas_call(
        boundary_kernel,
        grid=(steps,),
        out_shape=jax.ShapeDtypeStruct((peers, slots, width + LANES), BF16),
        in_specs=[
            pl.BlockSpec((bnd // steps, nodes), lambda i: (i, 0)),
            whole((nodes, width)),
        ],
        out_specs=pl.BlockSpec((peers // steps, slots, width + LANES), lambda i: (i, 0, 0)),
        compiler_params=PARAMS,
        cost_estimate=cost(bnd * nodes * width, 8 * MIB),
        name="boundary_grads",
    )(cbt, grad_agg)


def feats_grad_kernel(cot_ref, gagg_ref, gpre_ref, wst_ref, stale_ref, out_ref, token_ref):
    total = dot(gpre_ref[...], wst_ref[...]) + dot(cot_ref[...], gagg_ref[...])
    out_ref[...] = (total + stale_ref[...].astype(F32)).astype(BF16)
    token_ref[...] = jnp.zeros_like(token_ref)


def feats_grad(cot, grad_agg, grad_pre, w_self_t, stale_bgrad):
    nodes, width = grad_agg.shape
    block = 512
    by_block = lambda w: pl.BlockSpec((block, w), lambda i: (i, 0))
    return pl.pallas_call(
        feats_grad_kernel,
        grid=(nodes // block,),
        out_shape=[
            jax.ShapeDtypeStruct((nodes, width), BF16),
            jax.ShapeDtypeStruct((8, LANES), F32),
        ],
        in_specs=[
            by_block(nodes),
            whole((nodes, width)),
            by_block(width),
            whole((width, width)),
            by_block(width),
        ],
        out_specs=[by_block(width), whole((8, LANES))],
        compiler_params=PARAMS,
        cost_estimate=cost(nodes * width * (nodes + width), 7 * MIB),
        name="feats_grad",
    )(cot, grad_agg, grad_pre, w_self_t, stale_bgrad)


def add_kernel(keep_ref, got_ref, out_ref):
    out_ref[...] = (keep_ref[...] + got_ref[...].astype(F32)).astype(BF16)


def add_pair(keep, got):
    return pl.pallas_call(
        add_kernel,
        out_shape=jax.ShapeDtypeStruct(keep.shape, BF16),
        in_specs=[in_vmem()] * 2,
        out_specs=in_vmem(),
        compiler_params=SMALL_PARAMS,
        cost_estimate=cost(keep.size, 2 * MIB),
        name="add_pair",
    )(keep, got)


def take_kernel(ret_ref, _, out_ref):
    out_ref[...] = ret_ref[:, :, ret_ref.shape[2] - LANES :]


def take_shares(returned, token):
    peers, slots, _ = returned.shape
    return pl.pallas_call(
        take_kernel,
        out_shape=jax.ShapeDtypeStruct((peers, slots, LANES), BF16),
        in_specs=[in_vmem(), anywhere()],
        out_specs=in_vmem(),
        compiler_params=SMALL_PARAMS,
        cost_estimate=cost(peers * slots * LANES, MIB),
        name="take_shares",
    )(returned, token)


def sum_kernel(parts_ref, out_ref):
    total = parts_ref[0].astype(F32)
    for c in range(1, parts_ref.shape[0]):
        total += parts_ref[c].astype(F32)
    out_ref[...] = total.astype(BF16)


def sum_shares(parts):
    return pl.pallas_call(
        sum_kernel,
        out_shape=jax.ShapeDtypeStruct(parts.shape[1:], BF16),
        in_specs=[in_vmem()],
        out_specs=in_vmem(),
        compiler_params=SMALL_PARAMS,
        cost_estimate=cost(parts.size, MIB // 2),
        name="sum_shares",
    )(parts)


def lay_kernel(share_ref, _, out_ref, buf, sem):
    peers = buf.shape[0]
    for p in range(peers):
        buf[p] = share_ref[p % 2]
    width = out_ref.shape[2] - LANES
    copy = pltpu.make_async_copy(buf, out_ref.at[:, :, pl.ds(width, LANES)], sem)
    copy.start()
    copy.wait()


def lay_shares(share, rows):
    peers, slots, _ = rows.shape
    return pl.pallas_call(
        lay_kernel,
        out_shape=jax.ShapeDtypeStruct(rows.shape, BF16),
        in_specs=[in_vmem(), anywhere()],
        out_specs=anywhere(),
        scratch_shapes=[pltpu.VMEM((peers, slots, LANES), BF16), pltpu.SemaphoreType.DMA],
        input_output_aliases={1: 0},
        compiler_params=PARAMS,
        cost_estimate=cost(peers, MIB),
        name="lay_shares",
    )(share, rows)


def slots_by_lane(idx, lanes):
    slots, peers = idx.shape
    per = lanes // slots
    tall = jnp.concatenate([idx] * per, axis=0).T
    peer = lax.broadcasted_iota(jnp.int32, tall.shape, 0)
    lane = lax.broadcasted_iota(jnp.int32, tall.shape, 1)
    return jnp.where(peer % per == lane // slots, tall, 0).reshape(peers // per, per, lanes).sum(axis=1)


def scatter_kernel(idx_ref, cnt_ref, ret_ref, _, out_ref, *, chunks):
    peers, slots, _ = ret_ref.shape
    nodes, width = out_ref.shape
    per = peers // chunks
    idx = slots_by_lane(live_slots(idx_ref, cnt_ref), LANES)
    node_ids = lax.broadcasted_iota(jnp.int32, (nodes, LANES), 0)
    count = per * slots // LANES
    total = None
    for c in range(chunks):
        picks = [
            jnp.where(idx[n : n + 1, :] == node_ids, 1.0, 0.0).astype(BF16)
            for n in range(c * count, (c + 1) * count)
        ]
        rows = ret_ref[c * per : (c + 1) * per, :, :width].reshape(per * slots, width)
        term = dot(jnp.concatenate(picks, axis=1), rows)
        total = term if total is None else total + term
    out_ref[...] = total.astype(BF16)


def scatter(slot_rows, send_cnt, returned, token, nodes, chunks=4):
    width = returned.shape[2] - LANES
    return pl.pallas_call(
        functools.partial(scatter_kernel, chunks=chunks),
        out_shape=jax.ShapeDtypeStruct((nodes, width), BF16),
        in_specs=[in_vmem()] * 3 + [anywhere()],
        out_specs=in_vmem(),
        compiler_params=SMALL_PARAMS,
        cost_estimate=cost(returned.size * nodes, 4 * MIB),
        name="scatter_rows",
    )(slot_rows, send_cnt, returned, token)


def weights_kernel(core_ref, mine_ref, other_ref, ws_ref, wn_ref):
    first = core_ref[0] == 0
    chips, halves, rows, lanes = mine_ref.shape
    for part, out_ref in enumerate((ws_ref, wn_ref)):
        at = pl.ds(part * (chips // 2), chips // 2)
        for h in range(halves):
            mine = mine_ref[at, h].astype(F32).reshape(chips // 2 * rows, lanes)
            other = other_ref[at, h].astype(F32).reshape(chips // 2 * rows, lanes)
            out_ref[:, h * lanes : (h + 1) * lanes] = jnp.where(first, mine, other)
            out_ref[:, (2 + h) * lanes : (3 + h) * lanes] = jnp.where(first, other, mine)


def lay_weights(core, mine, other, width):
    return pl.pallas_call(
        weights_kernel,
        out_shape=[jax.ShapeDtypeStruct((width, width), F32)] * 2,
        in_specs=[scalars()] + [in_vmem()] * 2,
        out_specs=[in_vmem()] * 2,
        compiler_params=SMALL_PARAMS,
        cost_estimate=cost(width * width, 3 * MIB),
        name="lay_weights",
    )(core, mine, other)


def body(
    feats,
    stale_feats,
    grad_out,
    stale_bgrad,
    w_self,
    w_neigh,
    adj_tiles,
    tile_source_rows,
    tile_cnt,
    send_idx,
    send_cnt,
):
    peers, slots = send_idx.shape
    nodes, width = feats.shape
    tile_rows = adj_tiles.shape[2]
    all_tiles = (nodes + peers * slots) // tile_rows
    chips = peers // 2
    core = lax.rem(lax.axis_index("dom"), 2).astype(jnp.int32).reshape(1)
    pairs = [(d, d + 1 - 2 * (d % 2)) for d in range(peers)]
    same_core = [list(range(c, peers, 2)) for c in range(2)]

    def exchange(v, groups):
        return lax.all_to_all(
            v, "dom", split_axis=0, concat_axis=0, tiled=True, axis_index_groups=groups
        )

    slot_rows = send_idx.T
    outgoing = gather(slot_rows, send_cnt, stale_feats)
    incoming = exchange(outgoing, None).reshape(peers * slots, width)
    cb, cbt, cot, self_pre, own_agg, feats_t, w_self_t, w_neigh_t = combine(
        tile_source_rows, tile_cnt, adj_tiles, feats, w_self, w_neigh, all_tiles
    )
    activated, grad_pre, grad_agg, keep, give = layer(
        core, cb, incoming, self_pre, own_agg, grad_out, w_neigh, w_neigh_t, feats_t, chips
    )
    got = lax.ppermute(give, "dom", pairs)
    parts = exchange(add_pair(keep, got), same_core)
    rows = boundary(cbt, grad_agg, peers, slots)
    returned = exchange(lay_shares(sum_shares(parts), rows), None)
    grad_feats, token = feats_grad(cot, grad_agg, grad_pre, w_self_t, stale_bgrad)

    mine = take_shares(returned, token).reshape(keep.shape)
    other = lax.ppermute(mine, "dom", pairs)
    next_bgrad = scatter(slot_rows, send_cnt, returned, token, nodes)
    grad_w_self, grad_w_neigh = lay_weights(core, mine, other, width)
    return activated, grad_feats, next_bgrad, grad_w_self, grad_w_neigh


def solution(mesh):
    in_specs = (
        P("dom", None),
        P("dom", None),
        P("dom", None),
        P("dom", None),
        P(),
        P(),
        P("dom", None, None, None),
        P("dom", None),
        P("dom"),
        P("dom", None),
        P("dom", None),
    )
    out_specs = (P("dom", None), P("dom", None), P("dom", None), P(), P())
    return jax.shard_map(body, mesh=mesh, in_specs=in_specs, out_specs=out_specs, check_vma=False)
```

```python
import functools

import jax
import jax.numpy as jnp
from jax import lax
from jax.experimental import pallas as pl
from jax.experimental.pallas import tpu as pltpu
from jax.sharding import PartitionSpec as P

BF16 = jnp.bfloat16
F32 = jnp.float32
LANES = 128
MIB = 1 << 20
GELU_SLOPE = 0.7978845608028654
GELU_CUBIC = 0.044715


def dot(a, b):
    return jnp.dot(a, b, preferred_element_type=F32)


def whole(shape):
    return pl.BlockSpec(shape, lambda *_: (0,) * len(shape))


def scalars():
    return pl.BlockSpec(memory_space=pltpu.SMEM)


def anywhere():
    return pl.BlockSpec(memory_space=pl.ANY)


def in_vmem():
    return pl.BlockSpec(memory_space=pltpu.VMEM)


SMALL_PARAMS = pltpu.CompilerParams(vmem_limit_bytes=16 * MIB)
PARAMS = pltpu.CompilerParams(vmem_limit_bytes=56 * MIB)
LAYER_PARAMS = pltpu.CompilerParams(vmem_limit_bytes=48 * MIB)
LAY_PARAMS = pltpu.CompilerParams(vmem_limit_bytes=52 * MIB)


def cost(macs, moved):
    return pl.CostEstimate(flops=2 * macs, bytes_accessed=moved, transcendentals=0)


def live_slots(idx_ref, cnt_ref):
    live = lax.broadcasted_iota(jnp.int32, idx_ref.shape, 0) < cnt_ref[...]
    return jnp.where(live, idx_ref[...], -1)


def one_hot(idx, nodes, start, count):
    node_ids = lax.broadcasted_iota(jnp.int32, (idx.shape[0], nodes), 1)
    picks = [
        jnp.where(idx[:, t : t + 1] == node_ids, 1.0, 0.0).astype(BF16)
        for t in range(start, start + count)
    ]
    return jnp.concatenate(picks, axis=0)


def gather_kernel(idx_ref, cnt_ref, rows_ref, out_ref, rows, buf, sem, sems, *, groups):
    slots, peers = idx_ref.shape
    nodes, width = rows.shape
    load = pltpu.make_async_copy(rows_ref, rows, sem)
    load.start()
    idx = live_slots(idx_ref, cnt_ref)
    per = peers // groups
    copies = []
    for g in range(groups):
        picks = one_hot(idx, nodes, g * per, per)
        if g == 0:
            load.wait()
        span = pl.ds(g * per, per)
        buf[span] = dot(picks, rows[...]).astype(BF16).reshape(per, slots, width)
        copy = pltpu.make_async_copy(buf.at[span], out_ref.at[span], sems.at[g])
        copy.start()
        copies.append(copy)
    for copy in copies:
        copy.wait()


def gather(slot_rows, send_cnt, stale_feats, groups=8):
    slots, peers = slot_rows.shape
    nodes, width = stale_feats.shape
    return pl.pallas_call(
        functools.partial(gather_kernel, groups=groups),
        out_shape=jax.ShapeDtypeStruct((peers, slots, width), BF16),
        in_specs=[in_vmem()] * 2 + [anywhere()],
        out_specs=anywhere(),
        scratch_shapes=[
            pltpu.VMEM((nodes, width), BF16),
            pltpu.VMEM((peers, slots, width), BF16),
            pltpu.SemaphoreType.DMA,
            pltpu.SemaphoreType.DMA((groups,)),
        ],
        compiler_params=PARAMS,
        cost_estimate=cost(peers * slots * nodes * width, 3 * MIB),
        name="gather_rows",
    )(slot_rows, send_cnt, stale_feats)


def combine_kernel(
    src_ref, cnt_ref, adj_ref, feats_ref, ws_ref, wn_ref,
    cb_ref, cbt_ref, cot_ref, self_ref, own_ref, wst_ref, wnt_ref,
    acc,
):
    i = pl.program_id(0)
    tiles, rows = acc.shape[0], acc.shape[1]
    own_tiles = feats_ref.shape[0] // rows
    acc[...] = jnp.zeros_like(acc)

    @pl.when(i == 0)
    def _():
        wst_ref[...] = ws_ref[...].T
        wnt_ref[...] = wn_ref[...].T

    @pl.loop(0, cnt_ref[i])
    def _(j):
        s = src_ref[i, j]
        acc[s] += adj_ref[0, j].astype(F32)

    own = []
    for s in range(tiles):
        block = acc[s].astype(BF16)
        if s < own_tiles:
            own.append(block)
            cot_ref[s * rows : (s + 1) * rows, :] = block.T
        else:
            b = s - own_tiles
            cb_ref[:, b * rows : (b + 1) * rows] = block
            cbt_ref[b * rows : (b + 1) * rows, :] = block.T
    feats = feats_ref[...]
    own_ref[...] = dot(jnp.concatenate(own, axis=1), feats)
    mine = feats_ref[pl.ds(pl.multiple_of(i * rows, rows), rows), :]
    self_ref[...] = dot(mine, ws_ref[...])


def combine(tile_source_rows, tile_cnt, adj_tiles, feats, w_self, w_neigh, all_tiles):
    dst_tiles, slots, rows, _ = adj_tiles.shape
    nodes, width = feats.shape
    bnd = all_tiles * rows - nodes
    out_shape = [
        jax.ShapeDtypeStruct((nodes, bnd), BF16),
        jax.ShapeDtypeStruct((bnd, nodes), BF16),
        jax.ShapeDtypeStruct((nodes, nodes), BF16),
        jax.ShapeDtypeStruct((nodes, width), F32),
        jax.ShapeDtypeStruct((nodes, width), F32),
        jax.ShapeDtypeStruct((width, width), BF16),
        jax.ShapeDtypeStruct((width, width), BF16),
    ]
    return pl.pallas_call(
        combine_kernel,
        grid=(dst_tiles,),
        out_shape=out_shape,
        in_specs=[
            scalars(),
            scalars(),
            pl.BlockSpec((1, slots, rows, rows), lambda i: (i, 0, 0, 0)),
            whole((nodes, width)),
            whole((width, width)),
            whole((width, width)),
        ],
        out_specs=[
            pl.BlockSpec((rows, bnd), lambda i: (i, 0)),
            pl.BlockSpec((bnd, rows), lambda i: (0, i)),
            pl.BlockSpec((nodes, rows), lambda i: (0, i)),
            pl.BlockSpec((rows, width), lambda i: (i, 0)),
            pl.BlockSpec((rows, width), lambda i: (i, 0)),
            whole((width, width)),
            whole((width, width)),
        ],
        scratch_shapes=[pltpu.VMEM((all_tiles, rows, rows), F32)],
        compiler_params=PARAMS,
        cost_estimate=cost(nodes * width * (nodes + width), 20 * MIB),
        name="combine_tiles",
    )(tile_source_rows, tile_cnt, adj_tiles, feats, w_self, w_neigh)


class Stream:
    def __init__(self, copies, ahead):
        self.copies, self.ahead, self.started = copies, ahead, 0
        self.start(ahead)

    def start(self, count):
        while self.started < min(count, len(self.copies)):
            self.copies[self.started].start()
            self.started += 1

    def wait(self, *copies):
        for copy in copies:
            at = [c is copy for c in self.copies].index(True)
            self.start(at + 1 + self.ahead)
            copy.wait()


def layer_kernel(
    core_ref, cb_ref, in_ref, self_ref, own_ref, gout_ref, wn_ref, feats_ref,
    act_ref, gpre_ref, keep_ref, pass_ref,
    cb, rows_in, self_pre, own, gout, wn, feats, left, act, gpre, keep, give,
    cb_sems, in_sems, sems, out_sems,
):
    chunks = cb_sems.shape[0]
    bnd, width = rows_in.shape
    depth = bnd // chunks
    spans = [pl.ds(k * depth, depth) for k in range(chunks)]
    copy = pltpu.make_async_copy
    get_cb = [copy(cb_ref.at[:, d], cb.at[:, d], cb_sems.at[k]) for k, d in enumerate(spans)]
    get_in = [copy(in_ref.at[d], rows_in.at[d], in_sems.at[k]) for k, d in enumerate(spans)]
    rest = [
        (own_ref, own), (wn_ref, wn), (self_ref, self_pre), (gout_ref, gout),
        (feats_ref, feats),
    ]
    rest = [copy(src, dst, sems.at[n]) for n, (src, dst) in enumerate(rest)]
    loads = Stream([c for pair in zip(get_cb, get_in) for c in pair] + rest, 6)
    outs = []

    def put(src, dst):
        outs.append(copy(src, dst, out_sems.at[len(outs)]))
        outs[-1].start()

    total = None
    for k in range(chunks):
        loads.wait(get_cb[k], get_in[k])
        term = dot(cb[:, k * depth : (k + 1) * depth], rows_in[k * depth : (k + 1) * depth, :])
        total = term if total is None else total + term
    loads.wait(rest[0])
    agg = (total + own[...]).astype(BF16)
    loads.wait(rest[1], rest[2])
    pre = self_pre[...] + dot(agg, wn[...])
    left[width:, :] = agg.T
    square = pre * pre
    t = jnp.tanh(GELU_SLOPE * pre * (1.0 + GELU_CUBIC * square))
    half = 0.5 * (1.0 + t)
    act[...] = (pre * half).astype(BF16)
    slope = half + 0.5 * pre * (1.0 - t * t) * (
        GELU_SLOPE * (1.0 + (3.0 * GELU_CUBIC) * square)
    )
    loads.wait(rest[3])
    gpre[...] = (gout[...].astype(F32) * slope).astype(BF16)
    put(act, act_ref)
    put(gpre, gpre_ref)
    loads.wait(rest[4])
    left[:width, :] = feats[...].T
    first = core_ref[0] == 0
    groups, halves, rows, lanes = keep.shape
    g = dot(left[...], gpre[...]).reshape(groups, rows, width)
    for h in range(halves):
        even = g[:, :, 2 * h * lanes : (2 * h + 1) * lanes]
        odd = g[:, :, (2 * h + 1) * lanes : (2 * h + 2) * lanes]
        keep[:, h] = jnp.where(first, even, odd)
        give[:, h] = jnp.where(first, odd, even).astype(BF16)
    put(give, pass_ref)
    put(keep, keep_ref)
    for c in outs:
        c.wait()


def layer(core, cb, incoming, self_pre, own_agg, grad_out, w_neigh, feats, chips):
    nodes, bnd = cb.shape
    width = incoming.shape[1]
    chunks = 4
    shares = (chips, width // (2 * LANES), 2 * width // chips, LANES)
    vmem = pltpu.VMEM
    sems = pltpu.SemaphoreType.DMA
    return pl.pallas_call(
        layer_kernel,
        out_shape=[
            jax.ShapeDtypeStruct((nodes, width), BF16),
            jax.ShapeDtypeStruct((nodes, width), BF16),
            jax.ShapeDtypeStruct(shares, F32),
            jax.ShapeDtypeStruct(shares, BF16),
        ],
        in_specs=[scalars()] + [anywhere()] * 7,
        out_specs=[anywhere()] * 4,
        scratch_shapes=[
            vmem((nodes, bnd), BF16),
            vmem((bnd, width), BF16),
            vmem((nodes, width), F32),
            vmem((nodes, width), F32),
            vmem((nodes, width), BF16),
            vmem((width, width), BF16),
            vmem((nodes, width), BF16),
            vmem((2 * width, nodes), BF16),
            vmem((nodes, width), BF16),
            vmem((nodes, width), BF16),
            vmem(shares, F32),
            vmem(shares, BF16),
            sems((chunks,)),
            sems((chunks,)),
            sems((5,)),
            sems((4,)),
        ],
        compiler_params=LAYER_PARAMS,
        cost_estimate=cost(nodes * width * (bnd + 3 * width), 18 * MIB),
        name="layer",
    )(core, cb, incoming, self_pre, own_agg, grad_out, w_neigh, feats)


def boundary_kernel(cbt_ref, gpre_ref, wnt_ref, out_ref, gagg_ref):
    peers, slots, _ = out_ref.shape
    width = gagg_ref.shape[1]

    @pl.when(pl.program_id(0) == 0)
    def _():
        gagg_ref[...] = dot(gpre_ref[...], wnt_ref[...]).astype(BF16)

    got = dot(cbt_ref[...], gagg_ref[...]).astype(BF16)
    out_ref[:, :, :width] = got.reshape(peers, slots, width)


def boundary(cbt, grad_pre, w_neigh_t, peers, slots):
    bnd, nodes = cbt.shape
    width = grad_pre.shape[1]
    steps = 4
    return pl.pallas_call(
        boundary_kernel,
        grid=(steps,),
        out_shape=[
            jax.ShapeDtypeStruct((peers, slots, width + LANES), BF16),
            jax.ShapeDtypeStruct((nodes, width), BF16),
        ],
        in_specs=[
            pl.BlockSpec((bnd // steps, nodes), lambda i: (i, 0)),
            whole((nodes, width)),
            whole((width, width)),
        ],
        out_specs=[
            pl.BlockSpec((peers // steps, slots, width + LANES), lambda i: (i, 0, 0)),
            whole((nodes, width)),
        ],
        compiler_params=PARAMS,
        cost_estimate=cost((bnd + width) * nodes * width, 9 * MIB),
        name="boundary_grads",
    )(cbt, grad_pre, w_neigh_t)


def feats_grad_kernel(cot_ref, gagg_ref, gpre_ref, wst_ref, stale_ref, out_ref):
    total = dot(gpre_ref[...], wst_ref[...]) + dot(cot_ref[...], gagg_ref[...])
    out_ref[...] = (total + stale_ref[...].astype(F32)).astype(BF16)


def feats_grad(cot, grad_agg, grad_pre, w_self_t, stale_bgrad):
    nodes, width = grad_agg.shape
    block = 512
    by_block = lambda w: pl.BlockSpec((block, w), lambda i: (i, 0))
    return pl.pallas_call(
        feats_grad_kernel,
        grid=(nodes // block,),
        out_shape=jax.ShapeDtypeStruct((nodes, width), BF16),
        in_specs=[
            by_block(nodes),
            whole((nodes, width)),
            by_block(width),
            whole((width, width)),
            by_block(width),
        ],
        out_specs=by_block(width),
        compiler_params=PARAMS,
        cost_estimate=cost(nodes * width * (nodes + width), 7 * MIB),
        name="feats_grad",
    )(cot, grad_agg, grad_pre, w_self_t, stale_bgrad)


def add_kernel(keep_ref, got_ref, out_ref):
    out_ref[...] = (keep_ref[...] + got_ref[...].astype(F32)).astype(BF16)


def add_pair(keep, got):
    return pl.pallas_call(
        add_kernel,
        out_shape=jax.ShapeDtypeStruct(keep.shape, BF16),
        in_specs=[in_vmem()] * 2,
        out_specs=in_vmem(),
        compiler_params=SMALL_PARAMS,
        cost_estimate=cost(keep.size, 2 * MIB),
        name="add_pair",
    )(keep, got)


def take_kernel(ret_ref, out_ref):
    out_ref[...] = ret_ref[:, :, ret_ref.shape[2] - LANES :]


def take_shares(returned):
    peers, slots, _ = returned.shape
    return pl.pallas_call(
        take_kernel,
        out_shape=jax.ShapeDtypeStruct((peers, slots, LANES), BF16),
        in_specs=[in_vmem()],
        out_specs=in_vmem(),
        compiler_params=SMALL_PARAMS,
        cost_estimate=cost(peers * slots * LANES, MIB),
        name="take_shares",
    )(returned)


def share_kernel(parts_ref, _, out_ref, buf, sem):
    total = parts_ref[0].astype(F32)
    for c in range(1, parts_ref.shape[0]):
        total += parts_ref[c].astype(F32)
    total = total.astype(BF16)
    for p in range(buf.shape[0]):
        buf[p] = total[p % 2]
    width = out_ref.shape[2] - LANES
    copy = pltpu.make_async_copy(buf, out_ref.at[:, :, pl.ds(width, LANES)], sem)
    copy.start()
    copy.wait()


def lay_shares(parts, rows):
    peers, slots, _ = rows.shape
    return pl.pallas_call(
        share_kernel,
        out_shape=jax.ShapeDtypeStruct(rows.shape, BF16),
        in_specs=[in_vmem(), anywhere()],
        out_specs=anywhere(),
        scratch_shapes=[pltpu.VMEM((peers, slots, LANES), BF16), pltpu.SemaphoreType.DMA],
        input_output_aliases={1: 0},
        compiler_params=LAY_PARAMS,
        cost_estimate=cost(parts.size, MIB),
        name="lay_shares",
    )(parts, rows)


def slots_by_lane(idx, lanes):
    slots, peers = idx.shape
    per = lanes // slots
    tall = jnp.concatenate([idx] * per, axis=0).T
    peer = lax.broadcasted_iota(jnp.int32, tall.shape, 0)
    lane = lax.broadcasted_iota(jnp.int32, tall.shape, 1)
    return jnp.where(peer % per == lane // slots, tall, 0).reshape(peers // per, per, lanes).sum(axis=1)


def scatter_kernel(idx_ref, cnt_ref, ret_ref, out_ref, *, chunks):
    peers, slots, _ = ret_ref.shape
    nodes, width = out_ref.shape
    per = peers // chunks
    idx = slots_by_lane(live_slots(idx_ref, cnt_ref), LANES)
    node_ids = lax.broadcasted_iota(jnp.int32, (nodes, LANES), 0)
    count = per * slots // LANES
    total = None
    for c in range(chunks):
        picks = [
            jnp.where(idx[n : n + 1, :] == node_ids, 1.0, 0.0).astype(BF16)
            for n in range(c * count, (c + 1) * count)
        ]
        rows = ret_ref[c * per : (c + 1) * per, :, :width].reshape(per * slots, width)
        term = dot(jnp.concatenate(picks, axis=1), rows)
        total = term if total is None else total + term
    out_ref[...] = total.astype(BF16)


def scatter(slot_rows, send_cnt, returned, nodes, chunks=4):
    width = returned.shape[2] - LANES
    return pl.pallas_call(
        functools.partial(scatter_kernel, chunks=chunks),
        out_shape=jax.ShapeDtypeStruct((nodes, width), BF16),
        in_specs=[in_vmem()] * 3,
        out_specs=in_vmem(),
        compiler_params=SMALL_PARAMS,
        cost_estimate=cost(returned.size * nodes, 4 * MIB),
        name="scatter_rows",
    )(slot_rows, send_cnt, returned)


def weights_kernel(core_ref, mine_ref, other_ref, ws_ref, wn_ref):
    first = core_ref[0] == 0
    chips, halves, rows, lanes = mine_ref.shape
    for part, out_ref in enumerate((ws_ref, wn_ref)):
        at = pl.ds(part * (chips // 2), chips // 2)
        for h in range(halves):
            mine = mine_ref[at, h].astype(F32).reshape(chips // 2 * rows, lanes)
            other = other_ref[at, h].astype(F32).reshape(chips // 2 * rows, lanes)
            out_ref[:, h * lanes : (h + 1) * lanes] = jnp.where(first, mine, other)
            out_ref[:, (2 + h) * lanes : (3 + h) * lanes] = jnp.where(first, other, mine)


def lay_weights(core, mine, other, width):
    return pl.pallas_call(
        weights_kernel,
        out_shape=[jax.ShapeDtypeStruct((width, width), F32)] * 2,
        in_specs=[scalars()] + [in_vmem()] * 2,
        out_specs=[in_vmem()] * 2,
        compiler_params=SMALL_PARAMS,
        cost_estimate=cost(width * width, 3 * MIB),
        name="lay_weights",
    )(core, mine, other)


def body(
    feats,
    stale_feats,
    grad_out,
    stale_bgrad,
    w_self,
    w_neigh,
    adj_tiles,
    tile_source_rows,
    tile_cnt,
    send_idx,
    send_cnt,
):
    peers, slots = send_idx.shape
    nodes, width = feats.shape
    tile_rows = adj_tiles.shape[2]
    all_tiles = (nodes + peers * slots) // tile_rows
    chips = peers // 2
    core = lax.rem(lax.axis_index("dom"), 2).astype(jnp.int32).reshape(1)
    pairs = [(d, d + 1 - 2 * (d % 2)) for d in range(peers)]
    same_core = [list(range(c, peers, 2)) for c in range(2)]

    def exchange(v, groups):
        return lax.all_to_all(
            v, "dom", split_axis=0, concat_axis=0, tiled=True, axis_index_groups=groups
        )

    slot_rows = send_idx.T
    outgoing = gather(slot_rows, send_cnt, stale_feats)
    incoming = exchange(outgoing, None).reshape(peers * slots, width)
    cb, cbt, cot, self_pre, own_agg, w_self_t, w_neigh_t = combine(
        tile_source_rows, tile_cnt, adj_tiles, feats, w_self, w_neigh, all_tiles
    )
    activated, grad_pre, keep, give = layer(
        core, cb, incoming, self_pre, own_agg, grad_out, w_neigh, feats, chips
    )
    got = lax.ppermute(give, "dom", pairs)
    parts = exchange(add_pair(keep, got), same_core)
    rows, grad_agg = boundary(cbt, grad_pre, w_neigh_t, peers, slots)
    returned = exchange(lay_shares(parts, rows), None)
    grad_feats = feats_grad(cot, grad_agg, grad_pre, w_self_t, stale_bgrad)
    returned, grad_feats = lax.optimization_barrier((returned, grad_feats))

    mine = take_shares(returned).reshape(keep.shape)
    other = lax.ppermute(mine, "dom", pairs)
    next_bgrad = scatter(slot_rows, send_cnt, returned, nodes)
    grad_w_self, grad_w_neigh = lay_weights(core, mine, other, width)
    return activated, grad_feats, next_bgrad, grad_w_self, grad_w_neigh


def solution(mesh):
    in_specs = (
        P("dom", None),
        P("dom", None),
        P("dom", None),
        P("dom", None),
        P(),
        P(),
        P("dom", None, None, None),
        P("dom", None),
        P("dom"),
        P("dom", None),
        P("dom", None),
    )
    out_specs = (P("dom", None), P("dom", None), P("dom", None), P(), P())
    return jax.shard_map(body, mesh=mesh, in_specs=in_specs, out_specs=out_specs, check_vma=False)
```

```python
import functools

import jax
import jax.numpy as jnp
from jax import lax
from jax.experimental import pallas as pl
from jax.experimental.pallas import tpu as pltpu
from jax.sharding import PartitionSpec as P

BF16 = jnp.bfloat16
F32 = jnp.float32
LANES = 128
MIB = 1 << 20
GELU_SLOPE = 0.7978845608028654
GELU_CUBIC = 0.044715


def dot(a, b):
    return jnp.dot(a, b, preferred_element_type=F32)


def whole(shape):
    return pl.BlockSpec(shape, lambda *_: (0,) * len(shape))


def scalars():
    return pl.BlockSpec(memory_space=pltpu.SMEM)


def anywhere():
    return pl.BlockSpec(memory_space=pl.ANY)


def in_vmem():
    return pl.BlockSpec(memory_space=pltpu.VMEM)


SMALL_PARAMS = pltpu.CompilerParams(vmem_limit_bytes=16 * MIB)
PARAMS = pltpu.CompilerParams(vmem_limit_bytes=56 * MIB)
LAYER_PARAMS = pltpu.CompilerParams(vmem_limit_bytes=48 * MIB)
BACK_PARAMS = pltpu.CompilerParams(vmem_limit_bytes=56 * MIB)
LAY_PARAMS = pltpu.CompilerParams(vmem_limit_bytes=52 * MIB)


def cost(macs, moved):
    return pl.CostEstimate(flops=2 * macs, bytes_accessed=moved, transcendentals=0)


def live_slots(idx_ref, cnt_ref):
    live = lax.broadcasted_iota(jnp.int32, idx_ref.shape, 0) < cnt_ref[...]
    return jnp.where(live, idx_ref[...], -1)


def one_hot(idx, nodes, start, count):
    node_ids = lax.broadcasted_iota(jnp.int32, (idx.shape[0], nodes), 1)
    picks = [
        jnp.where(idx[:, t : t + 1] == node_ids, 1.0, 0.0).astype(BF16)
        for t in range(start, start + count)
    ]
    return jnp.concatenate(picks, axis=0)


def gather_kernel(idx_ref, cnt_ref, rows_ref, out_ref, rows, buf, sem, sems, *, groups):
    slots, peers = idx_ref.shape
    nodes, width = rows.shape
    load = pltpu.make_async_copy(rows_ref, rows, sem)
    load.start()
    idx = live_slots(idx_ref, cnt_ref)
    per = peers // groups
    copies = []
    for g in range(groups):
        picks = one_hot(idx, nodes, g * per, per)
        if g == 0:
            load.wait()
        span = pl.ds(g * per, per)
        buf[span] = dot(picks, rows[...]).astype(BF16).reshape(per, slots, width)
        copy = pltpu.make_async_copy(buf.at[span], out_ref.at[span], sems.at[g])
        copy.start()
        copies.append(copy)
    for copy in copies:
        copy.wait()


def gather(slot_rows, send_cnt, stale_feats, groups=8):
    slots, peers = slot_rows.shape
    nodes, width = stale_feats.shape
    return pl.pallas_call(
        functools.partial(gather_kernel, groups=groups),
        out_shape=jax.ShapeDtypeStruct((peers, slots, width), BF16),
        in_specs=[in_vmem()] * 2 + [anywhere()],
        out_specs=anywhere(),
        scratch_shapes=[
            pltpu.VMEM((nodes, width), BF16),
            pltpu.VMEM((peers, slots, width), BF16),
            pltpu.SemaphoreType.DMA,
            pltpu.SemaphoreType.DMA((groups,)),
        ],
        compiler_params=PARAMS,
        cost_estimate=cost(peers * slots * nodes * width, 3 * MIB),
        name="gather_rows",
    )(slot_rows, send_cnt, stale_feats)


def combine_kernel(
    src_ref, cnt_ref, adj_ref, feats_ref, ws_ref, wn_ref,
    cb_ref, cbt_ref, cot_ref, self_ref, own_ref, wst_ref, wnt_ref,
    acc,
):
    i = pl.program_id(0)
    tiles, rows = acc.shape[0], acc.shape[1]
    own_tiles = feats_ref.shape[0] // rows
    acc[...] = jnp.zeros_like(acc)

    @pl.when(i == 0)
    def _():
        wst_ref[...] = ws_ref[...].T
        wnt_ref[...] = wn_ref[...].T

    @pl.loop(0, cnt_ref[i])
    def _(j):
        s = src_ref[i, j]
        acc[s] += adj_ref[0, j].astype(F32)

    own = []
    for s in range(tiles):
        block = acc[s].astype(BF16)
        if s < own_tiles:
            own.append(block)
            cot_ref[s * rows : (s + 1) * rows, :] = block.T
        else:
            b = s - own_tiles
            cb_ref[:, b * rows : (b + 1) * rows] = block
            cbt_ref[b * rows : (b + 1) * rows, :] = block.T
    feats = feats_ref[...]
    own_ref[...] = dot(jnp.concatenate(own, axis=1), feats)
    mine = feats_ref[pl.ds(pl.multiple_of(i * rows, rows), rows), :]
    self_ref[...] = dot(mine, ws_ref[...])


def combine(tile_source_rows, tile_cnt, adj_tiles, feats, w_self, w_neigh, all_tiles):
    dst_tiles, slots, rows, _ = adj_tiles.shape
    nodes, width = feats.shape
    bnd = all_tiles * rows - nodes
    out_shape = [
        jax.ShapeDtypeStruct((nodes, bnd), BF16),
        jax.ShapeDtypeStruct((bnd, nodes), BF16),
        jax.ShapeDtypeStruct((nodes, nodes), BF16),
        jax.ShapeDtypeStruct((nodes, width), F32),
        jax.ShapeDtypeStruct((nodes, width), F32),
        jax.ShapeDtypeStruct((width, width), BF16),
        jax.ShapeDtypeStruct((width, width), BF16),
    ]
    return pl.pallas_call(
        combine_kernel,
        grid=(dst_tiles,),
        out_shape=out_shape,
        in_specs=[
            scalars(),
            scalars(),
            pl.BlockSpec((1, slots, rows, rows), lambda i: (i, 0, 0, 0)),
            whole((nodes, width)),
            whole((width, width)),
            whole((width, width)),
        ],
        out_specs=[
            pl.BlockSpec((rows, bnd), lambda i: (i, 0)),
            pl.BlockSpec((bnd, rows), lambda i: (0, i)),
            pl.BlockSpec((nodes, rows), lambda i: (0, i)),
            pl.BlockSpec((rows, width), lambda i: (i, 0)),
            pl.BlockSpec((rows, width), lambda i: (i, 0)),
            whole((width, width)),
            whole((width, width)),
        ],
        scratch_shapes=[pltpu.VMEM((all_tiles, rows, rows), F32)],
        compiler_params=PARAMS,
        cost_estimate=cost(nodes * width * (nodes + width), 20 * MIB),
        name="combine_tiles",
    )(tile_source_rows, tile_cnt, adj_tiles, feats, w_self, w_neigh)


class Stream:
    def __init__(self, copies, ahead):
        self.copies, self.ahead, self.started = copies, ahead, 0
        self.start(ahead)

    def start(self, count):
        while self.started < min(count, len(self.copies)):
            self.copies[self.started].start()
            self.started += 1

    def wait(self, *copies):
        for copy in copies:
            at = [c is copy for c in self.copies].index(True)
            self.start(at + 1 + self.ahead)
            copy.wait()


def layer_kernel(
    core_ref, cb_ref, in_ref, self_ref, own_ref, gout_ref, wn_ref, feats_ref,
    act_ref, gpre_ref, keep_ref, pass_ref,
    cb, rows_in, self_pre, own, gout, wn, feats, left, act, gpre, keep, give,
    cb_sems, in_sems, sems, out_sems,
):
    bnd, width = rows_in.shape
    cuts = [0, bnd // 8, bnd // 4, bnd // 2, 3 * bnd // 4, bnd]
    cuts = list(zip(cuts[:-1], cuts[1:]))
    spans = [pl.ds(a, b - a) for a, b in cuts]
    copy = pltpu.make_async_copy
    get_cb = [copy(cb_ref.at[:, d], cb.at[:, d], cb_sems.at[k]) for k, d in enumerate(spans)]
    get_in = [copy(in_ref.at[d], rows_in.at[d], in_sems.at[k]) for k, d in enumerate(spans)]
    rest = [
        (own_ref, own), (wn_ref, wn), (self_ref, self_pre), (gout_ref, gout),
        (feats_ref, feats),
    ]
    rest = [copy(src, dst, sems.at[n]) for n, (src, dst) in enumerate(rest)]
    loads = Stream([c for pair in zip(get_cb, get_in) for c in pair] + rest, 6)
    outs = []

    def put(src, dst):
        outs.append(copy(src, dst, out_sems.at[len(outs)]))
        outs[-1].start()

    total = None
    for k, (a, b) in enumerate(cuts):
        loads.wait(get_cb[k], get_in[k])
        term = dot(cb[:, a:b], rows_in[a:b, :])
        total = term if total is None else total + term
    loads.wait(rest[0])
    agg = (total + own[...]).astype(BF16)
    loads.wait(rest[1], rest[2])
    pre = self_pre[...] + dot(agg, wn[...])
    left[width:, :] = agg.T
    square = pre * pre
    t = jnp.tanh(GELU_SLOPE * pre * (1.0 + GELU_CUBIC * square))
    half = 0.5 * (1.0 + t)
    act[...] = (pre * half).astype(BF16)
    slope = half + 0.5 * pre * (1.0 - t * t) * (
        GELU_SLOPE * (1.0 + (3.0 * GELU_CUBIC) * square)
    )
    loads.wait(rest[3])
    gpre[...] = (gout[...].astype(F32) * slope).astype(BF16)
    put(act, act_ref)
    put(gpre, gpre_ref.at[0])
    loads.wait(rest[4])
    left[:width, :] = feats[...].T
    first = core_ref[0] == 0
    groups, halves, rows, lanes = keep.shape
    g = dot(left[...], gpre[...]).reshape(groups, rows, width)
    for h in range(halves):
        even = g[:, :, 2 * h * lanes : (2 * h + 1) * lanes]
        odd = g[:, :, (2 * h + 1) * lanes : (2 * h + 2) * lanes]
        keep[:, h] = jnp.where(first, even, odd)
        give[:, h] = jnp.where(first, odd, even).astype(BF16)
    put(give, pass_ref)
    put(keep, keep_ref)
    for c in outs:
        c.wait()


PLANES = 16


def layer(core, cb, incoming, self_pre, own_agg, grad_out, w_neigh, feats, chips):
    nodes, bnd = cb.shape
    width = incoming.shape[1]
    chunks = 5
    shares = (chips, width // (2 * LANES), 2 * width // chips, LANES)
    vmem = pltpu.VMEM
    sems = pltpu.SemaphoreType.DMA
    return pl.pallas_call(
        layer_kernel,
        out_shape=[
            jax.ShapeDtypeStruct((nodes, width), BF16),
            jax.ShapeDtypeStruct((PLANES, nodes, width), BF16),
            jax.ShapeDtypeStruct(shares, F32),
            jax.ShapeDtypeStruct(shares, BF16),
        ],
        in_specs=[scalars()] + [anywhere()] * 7,
        out_specs=[anywhere()] * 4,
        scratch_shapes=[
            vmem((nodes, bnd), BF16),
            vmem((bnd, width), BF16),
            vmem((nodes, width), F32),
            vmem((nodes, width), F32),
            vmem((nodes, width), BF16),
            vmem((width, width), BF16),
            vmem((nodes, width), BF16),
            vmem((2 * width, nodes), BF16),
            vmem((nodes, width), BF16),
            vmem((nodes, width), BF16),
            vmem(shares, F32),
            vmem(shares, BF16),
            sems((chunks,)),
            sems((chunks,)),
            sems((5,)),
            sems((4,)),
        ],
        compiler_params=LAYER_PARAMS,
        cost_estimate=cost(nodes * width * (bnd + 3 * width), 18 * MIB),
        name="layer",
    )(core, cb, incoming, self_pre, own_agg, grad_out, w_neigh, feats)


def boundary_kernel(
    cbt_ref, gpre_ref, wnt_ref, out_ref, gagg_ref,
    cbt, gpre, wnt, gagg, rows, cbt_sems, sems, out_sems,
):
    chunks = cbt_sems.shape[0]
    peers, slots, width = rows.shape
    nodes = gpre.shape[0]
    per, depth = peers // chunks, cbt.shape[0] // chunks
    copy = pltpu.make_async_copy
    get_w = copy(wnt_ref, wnt, sems.at[0])
    get_gpre = copy(gpre_ref.at[0], gpre, sems.at[1])
    get_cbt = [
        copy(cbt_ref.at[pl.ds(c * depth, depth)], cbt.at[pl.ds(c * depth, depth)], cbt_sems.at[c])
        for c in range(chunks)
    ]
    loads = Stream([get_w, get_gpre] + get_cbt, 3)
    outs = []

    def put(src, dst):
        outs.append(copy(src, dst, out_sems.at[len(outs)]))
        outs[-1].start()

    loads.wait(get_w, get_gpre)
    gagg[...] = dot(gpre[...], wnt[...]).astype(BF16)
    put(gagg, gagg_ref)
    for c in range(chunks):
        loads.wait(get_cbt[c])
        got = dot(cbt[c * depth : (c + 1) * depth, :], gagg[...]).astype(BF16)
        at = pl.ds(c * per, per)
        rows[at] = got.reshape(per, slots, width)
        put(rows.at[at], out_ref.at[at, :, pl.ds(0, width)])
    for c in outs:
        c.wait()


def boundary(cbt, grad_pre, w_neigh_t, peers, slots):
    bnd, nodes = cbt.shape
    width = grad_pre.shape[2]
    chunks = 4
    vmem = pltpu.VMEM
    return pl.pallas_call(
        boundary_kernel,
        out_shape=[
            jax.ShapeDtypeStruct((peers, slots, width + LANES), BF16),
            jax.ShapeDtypeStruct((nodes, width), BF16),
        ],
        in_specs=[anywhere()] * 3,
        out_specs=[anywhere()] * 2,
        scratch_shapes=[
            vmem((bnd, nodes), BF16),
            vmem((nodes, width), BF16),
            vmem((width, width), BF16),
            vmem((nodes, width), BF16),
            vmem((peers, slots, width), BF16),
            pltpu.SemaphoreType.DMA((chunks,)),
            pltpu.SemaphoreType.DMA((2,)),
            pltpu.SemaphoreType.DMA((chunks + 1,)),
        ],
        compiler_params=BACK_PARAMS,
        cost_estimate=cost((bnd + width) * nodes * width, 9 * MIB),
        name="boundary_grads",
    )(cbt, grad_pre, w_neigh_t)


def feats_grad_kernel(cot_ref, gagg_ref, gpre_ref, wst_ref, stale_ref, out_ref):
    total = dot(gpre_ref[0], wst_ref[...]) + dot(cot_ref[...], gagg_ref[...])
    out_ref[...] = (total + stale_ref[...].astype(F32)).astype(BF16)


def feats_grad(cot, grad_agg, grad_pre, w_self_t, stale_bgrad):
    nodes, width = grad_agg.shape
    block = 512
    by_block = lambda w: pl.BlockSpec((block, w), lambda i: (i, 0))
    return pl.pallas_call(
        feats_grad_kernel,
        grid=(nodes // block,),
        out_shape=jax.ShapeDtypeStruct((nodes, width), BF16),
        in_specs=[
            by_block(nodes),
            whole((nodes, width)),
            pl.BlockSpec((1, block, width), lambda i: (0, i, 0)),
            whole((width, width)),
            by_block(width),
        ],
        out_specs=by_block(width),
        compiler_params=PARAMS,
        cost_estimate=cost(nodes * width * (nodes + width), 7 * MIB),
        name="feats_grad",
    )(cot, grad_agg, grad_pre, w_self_t, stale_bgrad)


def add_kernel(keep_ref, got_ref, out_ref):
    out_ref[...] = (keep_ref[...] + got_ref[...].astype(F32)).astype(BF16)


def add_pair(keep, got):
    return pl.pallas_call(
        add_kernel,
        out_shape=jax.ShapeDtypeStruct(keep.shape, BF16),
        in_specs=[in_vmem()] * 2,
        out_specs=in_vmem(),
        compiler_params=SMALL_PARAMS,
        cost_estimate=cost(keep.size, 2 * MIB),
        name="add_pair",
    )(keep, got)


def take_kernel(ret_ref, out_ref):
    out_ref[...] = ret_ref[:, :, ret_ref.shape[2] - LANES :]


def take_shares(returned):
    peers, slots, _ = returned.shape
    return pl.pallas_call(
        take_kernel,
        out_shape=jax.ShapeDtypeStruct((peers, slots, LANES), BF16),
        in_specs=[in_vmem()],
        out_specs=in_vmem(),
        compiler_params=SMALL_PARAMS,
        cost_estimate=cost(peers * slots * LANES, MIB),
        name="take_shares",
    )(returned)


def share_kernel(parts_ref, _, out_ref, buf, sem):
    total = parts_ref[0].astype(F32)
    for c in range(1, parts_ref.shape[0]):
        total += parts_ref[c].astype(F32)
    total = total.astype(BF16)
    for p in range(buf.shape[0]):
        buf[p] = total[p % 2]
    width = out_ref.shape[2] - LANES
    copy = pltpu.make_async_copy(buf, out_ref.at[:, :, pl.ds(width, LANES)], sem)
    copy.start()
    copy.wait()


def lay_shares(parts, rows):
    peers, slots, _ = rows.shape
    return pl.pallas_call(
        share_kernel,
        out_shape=jax.ShapeDtypeStruct(rows.shape, BF16),
        in_specs=[in_vmem(), anywhere()],
        out_specs=anywhere(),
        scratch_shapes=[pltpu.VMEM((peers, slots, LANES), BF16), pltpu.SemaphoreType.DMA],
        input_output_aliases={1: 0},
        compiler_params=LAY_PARAMS,
        cost_estimate=cost(parts.size, MIB),
        name="lay_shares",
    )(parts, rows)


def slots_by_lane(idx, lanes):
    slots, peers = idx.shape
    per = lanes // slots
    tall = jnp.concatenate([idx] * per, axis=0).T
    peer = lax.broadcasted_iota(jnp.int32, tall.shape, 0)
    lane = lax.broadcasted_iota(jnp.int32, tall.shape, 1)
    return jnp.where(peer % per == lane // slots, tall, 0).reshape(peers // per, per, lanes).sum(axis=1)


def scatter_kernel(idx_ref, cnt_ref, ret_ref, out_ref, *, chunks):
    peers, slots, _ = ret_ref.shape
    nodes, width = out_ref.shape
    per = peers // chunks
    idx = slots_by_lane(live_slots(idx_ref, cnt_ref), LANES)
    node_ids = lax.broadcasted_iota(jnp.int32, (nodes, LANES), 0)
    count = per * slots // LANES
    total = None
    for c in range(chunks):
        picks = [
            jnp.where(idx[n : n + 1, :] == node_ids, 1.0, 0.0).astype(BF16)
            for n in range(c * count, (c + 1) * count)
        ]
        rows = ret_ref[c * per : (c + 1) * per, :, :width].reshape(per * slots, width)
        term = dot(jnp.concatenate(picks, axis=1), rows)
        total = term if total is None else total + term
    out_ref[...] = total.astype(BF16)


def scatter(slot_rows, send_cnt, returned, nodes, chunks=4):
    width = returned.shape[2] - LANES
    return pl.pallas_call(
        functools.partial(scatter_kernel, chunks=chunks),
        out_shape=jax.ShapeDtypeStruct((nodes, width), BF16),
        in_specs=[in_vmem()] * 3,
        out_specs=in_vmem(),
        compiler_params=SMALL_PARAMS,
        cost_estimate=cost(returned.size * nodes, 4 * MIB),
        name="scatter_rows",
    )(slot_rows, send_cnt, returned)


def weights_kernel(core_ref, mine_ref, other_ref, ws_ref, wn_ref):
    first = core_ref[0] == 0
    chips, halves, rows, lanes = mine_ref.shape
    for part, out_ref in enumerate((ws_ref, wn_ref)):
        at = pl.ds(part * (chips // 2), chips // 2)
        for h in range(halves):
            mine = mine_ref[at, h].astype(F32).reshape(chips // 2 * rows, lanes)
            other = other_ref[at, h].astype(F32).reshape(chips // 2 * rows, lanes)
            out_ref[:, h * lanes : (h + 1) * lanes] = jnp.where(first, mine, other)
            out_ref[:, (2 + h) * lanes : (3 + h) * lanes] = jnp.where(first, other, mine)


def lay_weights(core, mine, other, width):
    return pl.pallas_call(
        weights_kernel,
        out_shape=[jax.ShapeDtypeStruct((width, width), F32)] * 2,
        in_specs=[scalars()] + [in_vmem()] * 2,
        out_specs=[in_vmem()] * 2,
        compiler_params=SMALL_PARAMS,
        cost_estimate=cost(width * width, 3 * MIB),
        name="lay_weights",
    )(core, mine, other)


def body(
    feats,
    stale_feats,
    grad_out,
    stale_bgrad,
    w_self,
    w_neigh,
    adj_tiles,
    tile_source_rows,
    tile_cnt,
    send_idx,
    send_cnt,
):
    peers, slots = send_idx.shape
    nodes, width = feats.shape
    tile_rows = adj_tiles.shape[2]
    all_tiles = (nodes + peers * slots) // tile_rows
    chips = peers // 2
    core = lax.rem(lax.axis_index("dom"), 2).astype(jnp.int32).reshape(1)
    pairs = [(d, d + 1 - 2 * (d % 2)) for d in range(peers)]
    same_core = [list(range(c, peers, 2)) for c in range(2)]

    def exchange(v, groups):
        return lax.all_to_all(
            v, "dom", split_axis=0, concat_axis=0, tiled=True, axis_index_groups=groups
        )

    slot_rows = send_idx.T
    outgoing = gather(slot_rows, send_cnt, stale_feats)
    incoming = exchange(outgoing, None).reshape(peers * slots, width)
    cb, cbt, cot, self_pre, own_agg, w_self_t, w_neigh_t = combine(
        tile_source_rows, tile_cnt, adj_tiles, feats, w_self, w_neigh, all_tiles
    )
    activated, grad_pre, keep, give = layer(
        core, cb, incoming, self_pre, own_agg, grad_out, w_neigh, feats, chips
    )
    got = lax.ppermute(give, "dom", pairs)
    parts = exchange(add_pair(keep, got), same_core)
    rows, grad_agg = boundary(cbt, grad_pre, w_neigh_t, peers, slots)
    returned = exchange(lay_shares(parts, rows), None)
    grad_feats = feats_grad(cot, grad_agg, grad_pre, w_self_t, stale_bgrad)
    returned, grad_feats = lax.optimization_barrier((returned, grad_feats))

    mine = take_shares(returned).reshape(keep.shape)
    other = lax.ppermute(mine, "dom", pairs)
    next_bgrad = scatter(slot_rows, send_cnt, returned, nodes)
    grad_w_self, grad_w_neigh = lay_weights(core, mine, other, width)
    return activated, grad_feats, next_bgrad, grad_w_self, grad_w_neigh


def solution(mesh):
    in_specs = (
        P("dom", None),
        P("dom", None),
        P("dom", None),
        P("dom", None),
        P(),
        P(),
        P("dom", None, None, None),
        P("dom", None),
        P("dom"),
        P("dom", None),
        P("dom", None),
    )
    out_specs = (P("dom", None), P("dom", None), P("dom", None), P(), P())
    return jax.shard_map(body, mesh=mesh, in_specs=in_specs, out_specs=out_specs, check_vma=False)
```

```python
import functools

import jax
import jax.numpy as jnp
from jax import lax
from jax.experimental import pallas as pl
from jax.experimental.pallas import tpu as pltpu
from jax.sharding import PartitionSpec as P

BF16 = jnp.bfloat16
F32 = jnp.float32
LANES = 128
MIB = 1 << 20
GELU_SLOPE = 0.7978845608028654
GELU_CUBIC = 0.044715


def dot(a, b):
    return jnp.dot(a, b, preferred_element_type=F32)


def whole(shape):
    return pl.BlockSpec(shape, lambda *_: (0,) * len(shape))


def scalars():
    return pl.BlockSpec(memory_space=pltpu.SMEM)


def anywhere():
    return pl.BlockSpec(memory_space=pl.ANY)


def in_vmem():
    return pl.BlockSpec(memory_space=pltpu.VMEM)


SMALL_PARAMS = pltpu.CompilerParams(vmem_limit_bytes=16 * MIB)
PARAMS = pltpu.CompilerParams(vmem_limit_bytes=56 * MIB)
LAYER_PARAMS = pltpu.CompilerParams(vmem_limit_bytes=48 * MIB)
BACK_PARAMS = pltpu.CompilerParams(vmem_limit_bytes=56 * MIB)
LAY_PARAMS = pltpu.CompilerParams(vmem_limit_bytes=52 * MIB)


def cost(macs, moved):
    return pl.CostEstimate(flops=2 * macs, bytes_accessed=moved, transcendentals=0)


def first_core():
    return lax.rem(lax.axis_index("dom"), 2) == 0


def live_slots(idx_ref, cnt_ref):
    live = lax.broadcasted_iota(jnp.int32, idx_ref.shape, 0) < cnt_ref[...]
    return jnp.where(live, idx_ref[...], -1)


def one_hot(idx, nodes, start, count):
    node_ids = lax.broadcasted_iota(jnp.int32, (idx.shape[0], nodes), 1)
    picks = [
        jnp.where(idx[:, t : t + 1] == node_ids, 1.0, 0.0).astype(BF16)
        for t in range(start, start + count)
    ]
    return jnp.concatenate(picks, axis=0)


def gather_kernel(
    idx_ref, cnt_ref, rows_ref, out_ref, slot_idx, slot_cnt, rows, buf, load_sems, sems
):
    groups = sems.shape[0]
    slots, peers = slot_idx.shape
    nodes, width = rows.shape
    pairs = ((idx_ref, slot_idx), (cnt_ref, slot_cnt), (rows_ref, rows))
    loads = [
        pltpu.make_async_copy(src, dst, load_sems.at[n]) for n, (src, dst) in enumerate(pairs)
    ]
    for load in loads:
        load.start()
    loads[0].wait()
    loads[1].wait()
    idx = live_slots(slot_idx, slot_cnt)
    per = peers // groups
    copies = []
    for g in range(groups):
        picks = one_hot(idx, nodes, g * per, per)
        if g == 0:
            loads[2].wait()
        span = pl.ds(g * per, per)
        buf[span] = dot(picks, rows[...]).astype(BF16).reshape(per, slots, width)
        copy = pltpu.make_async_copy(buf.at[span], out_ref.at[span], sems.at[g])
        copy.start()
        copies.append(copy)
    for copy in copies:
        copy.wait()


def gather(slot_rows, send_cnt, stale_feats, groups=8):
    slots, peers = slot_rows.shape
    nodes, width = stale_feats.shape
    return pl.pallas_call(
        gather_kernel,
        out_shape=jax.ShapeDtypeStruct((peers, slots, width), BF16),
        in_specs=[anywhere()] * 3,
        out_specs=anywhere(),
        scratch_shapes=[
            pltpu.VMEM((slots, peers), jnp.int32),
            pltpu.VMEM((1, peers), jnp.int32),
            pltpu.VMEM((nodes, width), BF16),
            pltpu.VMEM((peers, slots, width), BF16),
            pltpu.SemaphoreType.DMA((3,)),
            pltpu.SemaphoreType.DMA((groups,)),
        ],
        compiler_params=PARAMS,
        cost_estimate=cost(peers * slots * nodes * width, 3 * MIB),
        name="gather_rows",
    )(slot_rows, send_cnt, stale_feats)


def combine_kernel(
    src_ref, cnt_ref, adj_ref, feats_ref, ws_ref, wn_ref,
    cb_ref, cbt_ref, cot_ref, self_ref, own_ref, wst_ref, wnt_ref,
    acc,
):
    i = pl.program_id(0)
    tiles, rows = acc.shape[0], acc.shape[1]
    own_tiles = feats_ref.shape[0] // rows
    acc[...] = jnp.zeros_like(acc)

    @pl.when(i == 0)
    def _():
        wst_ref[...] = ws_ref[...].T
        wnt_ref[...] = wn_ref[...].T

    @pl.loop(0, cnt_ref[i])
    def _(j):
        s = src_ref[i, j]
        acc[s] += adj_ref[0, j].astype(F32)

    own = []
    for s in range(tiles):
        block = acc[s].astype(BF16)
        if s < own_tiles:
            own.append(block)
            cot_ref[s * rows : (s + 1) * rows, :] = block.T
        else:
            b = s - own_tiles
            cb_ref[:, b * rows : (b + 1) * rows] = block
            cbt_ref[b * rows : (b + 1) * rows, :] = block.T
    feats = feats_ref[...]
    own_ref[...] = dot(jnp.concatenate(own, axis=1), feats)
    mine = feats_ref[pl.ds(pl.multiple_of(i * rows, rows), rows), :]
    self_ref[...] = dot(mine, ws_ref[...])


def combine(tile_source_rows, tile_cnt, adj_tiles, feats, w_self, w_neigh, all_tiles):
    dst_tiles, slots, rows, _ = adj_tiles.shape
    nodes, width = feats.shape
    bnd = all_tiles * rows - nodes
    out_shape = [
        jax.ShapeDtypeStruct((nodes, bnd), BF16),
        jax.ShapeDtypeStruct((bnd, nodes), BF16),
        jax.ShapeDtypeStruct((nodes, nodes), BF16),
        jax.ShapeDtypeStruct((nodes, width), F32),
        jax.ShapeDtypeStruct((nodes, width), F32),
        jax.ShapeDtypeStruct((width, width), BF16),
        jax.ShapeDtypeStruct((width, width), BF16),
    ]
    return pl.pallas_call(
        combine_kernel,
        grid=(dst_tiles,),
        out_shape=out_shape,
        in_specs=[
            scalars(),
            scalars(),
            pl.BlockSpec((1, slots, rows, rows), lambda i: (i, 0, 0, 0)),
            whole((nodes, width)),
            whole((width, width)),
            whole((width, width)),
        ],
        out_specs=[
            pl.BlockSpec((rows, bnd), lambda i: (i, 0)),
            pl.BlockSpec((bnd, rows), lambda i: (0, i)),
            pl.BlockSpec((nodes, rows), lambda i: (0, i)),
            pl.BlockSpec((rows, width), lambda i: (i, 0)),
            pl.BlockSpec((rows, width), lambda i: (i, 0)),
            whole((width, width)),
            whole((width, width)),
        ],
        scratch_shapes=[pltpu.VMEM((all_tiles, rows, rows), F32)],
        compiler_params=PARAMS,
        cost_estimate=cost(nodes * width * (nodes + width), 20 * MIB),
        name="combine_tiles",
    )(tile_source_rows, tile_cnt, adj_tiles, feats, w_self, w_neigh)


class Stream:
    def __init__(self, copies, ahead):
        self.copies, self.ahead, self.started = copies, ahead, 0
        self.start(ahead)

    def start(self, count):
        while self.started < min(count, len(self.copies)):
            self.copies[self.started].start()
            self.started += 1

    def wait(self, *copies):
        for copy in copies:
            at = [c is copy for c in self.copies].index(True)
            self.start(at + 1 + self.ahead)
            copy.wait()


def layer_kernel(
    cb_ref, in_ref, self_ref, own_ref, gout_ref, wn_ref, feats_ref,
    act_ref, gpre_ref, keep_ref, pass_ref,
    cb, rows_in, self_pre, own, gout, wn, feats, left, act, gpre, keep, give,
    cb_sems, in_sems, sems, out_sems,
):
    bnd, width = rows_in.shape
    cuts = [0, bnd // 8, bnd // 4, bnd // 2, 3 * bnd // 4, bnd]
    cuts = list(zip(cuts[:-1], cuts[1:]))
    spans = [pl.ds(a, b - a) for a, b in cuts]
    copy = pltpu.make_async_copy
    get_cb = [copy(cb_ref.at[:, d], cb.at[:, d], cb_sems.at[k]) for k, d in enumerate(spans)]
    get_in = [copy(in_ref.at[d], rows_in.at[d], in_sems.at[k]) for k, d in enumerate(spans)]
    rest = [
        (own_ref, own), (wn_ref, wn), (self_ref, self_pre), (gout_ref, gout),
        (feats_ref, feats),
    ]
    rest = [copy(src, dst, sems.at[n]) for n, (src, dst) in enumerate(rest)]
    loads = Stream([c for pair in zip(get_cb, get_in) for c in pair] + rest, 6)
    outs = []

    def put(src, dst):
        outs.append(copy(src, dst, out_sems.at[len(outs)]))
        outs[-1].start()

    total = None
    for k, (a, b) in enumerate(cuts):
        loads.wait(get_cb[k], get_in[k])
        term = dot(cb[:, a:b], rows_in[a:b, :])
        total = term if total is None else total + term
    loads.wait(rest[0])
    agg = (total + own[...]).astype(BF16)
    loads.wait(rest[1], rest[2])
    pre = self_pre[...] + dot(agg, wn[...])
    left[width:, :] = agg.T
    square = pre * pre
    t = jnp.tanh(GELU_SLOPE * pre * (1.0 + GELU_CUBIC * square))
    half = 0.5 * (1.0 + t)
    act[...] = (pre * half).astype(BF16)
    slope = half + 0.5 * pre * (1.0 - t * t) * (
        GELU_SLOPE * (1.0 + (3.0 * GELU_CUBIC) * square)
    )
    loads.wait(rest[3])
    gpre[...] = (gout[...].astype(F32) * slope).astype(BF16)
    put(act, act_ref)
    put(gpre, gpre_ref.at[0])
    loads.wait(rest[4])
    left[:width, :] = feats[...].T
    first = first_core()
    groups, halves, rows, lanes = keep.shape
    g = dot(left[...], gpre[...]).reshape(groups, rows, width)
    for h in range(halves):
        even = g[:, :, 2 * h * lanes : (2 * h + 1) * lanes]
        odd = g[:, :, (2 * h + 1) * lanes : (2 * h + 2) * lanes]
        keep[:, h] = jnp.where(first, even, odd)
        give[:, h] = jnp.where(first, odd, even).astype(BF16)
    put(give, pass_ref)
    put(keep, keep_ref)
    for c in outs:
        c.wait()


PLANES = 16


def layer(cb, incoming, self_pre, own_agg, grad_out, w_neigh, feats, chips):
    nodes, bnd = cb.shape
    width = incoming.shape[1]
    chunks = 5
    shares = (chips, width // (2 * LANES), 2 * width // chips, LANES)
    vmem = pltpu.VMEM
    sems = pltpu.SemaphoreType.DMA
    return pl.pallas_call(
        layer_kernel,
        out_shape=[
            jax.ShapeDtypeStruct((nodes, width), BF16),
            jax.ShapeDtypeStruct((PLANES, nodes, width), BF16),
            jax.ShapeDtypeStruct(shares, F32),
            jax.ShapeDtypeStruct(shares, BF16),
        ],
        in_specs=[anywhere()] * 7,
        out_specs=[anywhere()] * 4,
        scratch_shapes=[
            vmem((nodes, bnd), BF16),
            vmem((bnd, width), BF16),
            vmem((nodes, width), F32),
            vmem((nodes, width), F32),
            vmem((nodes, width), BF16),
            vmem((width, width), BF16),
            vmem((nodes, width), BF16),
            vmem((2 * width, nodes), BF16),
            vmem((nodes, width), BF16),
            vmem((nodes, width), BF16),
            vmem(shares, F32),
            vmem(shares, BF16),
            sems((chunks,)),
            sems((chunks,)),
            sems((5,)),
            sems((4,)),
        ],
        compiler_params=LAYER_PARAMS,
        cost_estimate=cost(nodes * width * (bnd + 3 * width), 18 * MIB),
        name="layer",
    )(cb, incoming, self_pre, own_agg, grad_out, w_neigh, feats)


def boundary_kernel(
    cbt_ref, gpre_ref, wnt_ref, out_ref, gagg_ref,
    cbt, gpre, wnt, gagg, rows, cbt_sems, sems, out_sems,
):
    chunks = cbt_sems.shape[0]
    peers, slots, width = rows.shape
    nodes = gpre.shape[0]
    per, depth = peers // chunks, cbt.shape[0] // chunks
    copy = pltpu.make_async_copy
    get_w = copy(wnt_ref, wnt, sems.at[0])
    get_gpre = copy(gpre_ref.at[0], gpre, sems.at[1])
    get_cbt = [
        copy(cbt_ref.at[pl.ds(c * depth, depth)], cbt.at[pl.ds(c * depth, depth)], cbt_sems.at[c])
        for c in range(chunks)
    ]
    loads = Stream([get_w, get_gpre] + get_cbt, 3)
    outs = []

    def put(src, dst):
        outs.append(copy(src, dst, out_sems.at[len(outs)]))
        outs[-1].start()

    loads.wait(get_w, get_gpre)
    gagg[...] = dot(gpre[...], wnt[...]).astype(BF16)
    put(gagg, gagg_ref)
    for c in range(chunks):
        loads.wait(get_cbt[c])
        got = dot(cbt[c * depth : (c + 1) * depth, :], gagg[...]).astype(BF16)
        at = pl.ds(c * per, per)
        rows[at] = got.reshape(per, slots, width)
        put(rows.at[at], out_ref.at[at, :, pl.ds(0, width)])
    for c in outs:
        c.wait()


def boundary(cbt, grad_pre, w_neigh_t, peers, slots):
    bnd, nodes = cbt.shape
    width = grad_pre.shape[2]
    chunks = 4
    vmem = pltpu.VMEM
    return pl.pallas_call(
        boundary_kernel,
        out_shape=[
            jax.ShapeDtypeStruct((peers, slots, width + LANES), BF16),
            jax.ShapeDtypeStruct((nodes, width), BF16),
        ],
        in_specs=[anywhere()] * 3,
        out_specs=[anywhere()] * 2,
        scratch_shapes=[
            vmem((bnd, nodes), BF16),
            vmem((nodes, width), BF16),
            vmem((width, width), BF16),
            vmem((nodes, width), BF16),
            vmem((peers, slots, width), BF16),
            pltpu.SemaphoreType.DMA((chunks,)),
            pltpu.SemaphoreType.DMA((2,)),
            pltpu.SemaphoreType.DMA((chunks + 1,)),
        ],
        compiler_params=BACK_PARAMS,
        cost_estimate=cost((bnd + width) * nodes * width, 9 * MIB),
        name="boundary_grads",
    )(cbt, grad_pre, w_neigh_t)


def feats_grad_kernel(cot_ref, gagg_ref, gpre_ref, wst_ref, stale_ref, out_ref):
    total = dot(gpre_ref[0], wst_ref[...]) + dot(cot_ref[...], gagg_ref[...])
    out_ref[...] = (total + stale_ref[...].astype(F32)).astype(BF16)


def feats_grad(cot, grad_agg, grad_pre, w_self_t, stale_bgrad):
    nodes, width = grad_agg.shape
    block = 512
    by_block = lambda w: pl.BlockSpec((block, w), lambda i: (i, 0))
    return pl.pallas_call(
        feats_grad_kernel,
        grid=(nodes // block,),
        out_shape=jax.ShapeDtypeStruct((nodes, width), BF16),
        in_specs=[
            by_block(nodes),
            whole((nodes, width)),
            pl.BlockSpec((1, block, width), lambda i: (0, i, 0)),
            whole((width, width)),
            by_block(width),
        ],
        out_specs=by_block(width),
        compiler_params=PARAMS,
        cost_estimate=cost(nodes * width * (nodes + width), 7 * MIB),
        name="feats_grad",
    )(cot, grad_agg, grad_pre, w_self_t, stale_bgrad)


def add_kernel(keep_ref, got_ref, out_ref):
    out_ref[...] = (keep_ref[...] + got_ref[...].astype(F32)).astype(BF16)


def add_pair(keep, got):
    return pl.pallas_call(
        add_kernel,
        out_shape=jax.ShapeDtypeStruct(keep.shape, BF16),
        in_specs=[in_vmem()] * 2,
        out_specs=in_vmem(),
        compiler_params=SMALL_PARAMS,
        cost_estimate=cost(keep.size, 2 * MIB),
        name="add_pair",
    )(keep, got)


def take_kernel(ret_ref, out_ref):
    out_ref[...] = ret_ref[:, :, ret_ref.shape[2] - LANES :]


def take_shares(returned):
    peers, slots, _ = returned.shape
    return pl.pallas_call(
        take_kernel,
        out_shape=jax.ShapeDtypeStruct((peers, slots, LANES), BF16),
        in_specs=[in_vmem()],
        out_specs=in_vmem(),
        compiler_params=SMALL_PARAMS,
        cost_estimate=cost(peers * slots * LANES, MIB),
        name="take_shares",
    )(returned)


def share_kernel(parts_ref, _, out_ref, buf, sem):
    total = parts_ref[0].astype(F32)
    for c in range(1, parts_ref.shape[0]):
        total += parts_ref[c].astype(F32)
    total = total.astype(BF16)
    for p in range(buf.shape[0]):
        buf[p] = total[p % 2]
    width = out_ref.shape[2] - LANES
    copy = pltpu.make_async_copy(buf, out_ref.at[:, :, pl.ds(width, LANES)], sem)
    copy.start()
    copy.wait()


def lay_shares(parts, rows):
    peers, slots, _ = rows.shape
    return pl.pallas_call(
        share_kernel,
        out_shape=jax.ShapeDtypeStruct(rows.shape, BF16),
        in_specs=[in_vmem(), anywhere()],
        out_specs=anywhere(),
        scratch_shapes=[pltpu.VMEM((peers, slots, LANES), BF16), pltpu.SemaphoreType.DMA],
        input_output_aliases={1: 0},
        compiler_params=LAY_PARAMS,
        cost_estimate=cost(parts.size, MIB),
        name="lay_shares",
    )(parts, rows)


def slots_by_lane(idx, lanes):
    slots, peers = idx.shape
    per = lanes // slots
    tall = jnp.concatenate([idx] * per, axis=0).T
    peer = lax.broadcasted_iota(jnp.int32, tall.shape, 0)
    lane = lax.broadcasted_iota(jnp.int32, tall.shape, 1)
    return jnp.where(peer % per == lane // slots, tall, 0).reshape(peers // per, per, lanes).sum(axis=1)


def scatter_kernel(idx_ref, cnt_ref, ret_ref, out_ref, *, chunks):
    peers, slots, _ = ret_ref.shape
    nodes, width = out_ref.shape
    per = peers // chunks
    idx = slots_by_lane(live_slots(idx_ref, cnt_ref), LANES)
    node_ids = lax.broadcasted_iota(jnp.int32, (nodes, LANES), 0)
    count = per * slots // LANES
    total = None
    for c in range(chunks):
        picks = [
            jnp.where(idx[n : n + 1, :] == node_ids, 1.0, 0.0).astype(BF16)
            for n in range(c * count, (c + 1) * count)
        ]
        rows = ret_ref[c * per : (c + 1) * per, :, :width].reshape(per * slots, width)
        term = dot(jnp.concatenate(picks, axis=1), rows)
        total = term if total is None else total + term
    out_ref[...] = total.astype(BF16)


def scatter(slot_rows, send_cnt, returned, nodes, chunks=4):
    width = returned.shape[2] - LANES
    return pl.pallas_call(
        functools.partial(scatter_kernel, chunks=chunks),
        out_shape=jax.ShapeDtypeStruct((nodes, width), BF16),
        in_specs=[in_vmem()] * 3,
        out_specs=in_vmem(),
        compiler_params=SMALL_PARAMS,
        cost_estimate=cost(returned.size * nodes, 4 * MIB),
        name="scatter_rows",
    )(slot_rows, send_cnt, returned)


def weights_kernel(mine_ref, other_ref, ws_ref, wn_ref):
    first = first_core()
    chips, halves, rows, lanes = mine_ref.shape
    for part, out_ref in enumerate((ws_ref, wn_ref)):
        at = pl.ds(part * (chips // 2), chips // 2)
        for h in range(halves):
            mine = mine_ref[at, h].astype(F32).reshape(chips // 2 * rows, lanes)
            other = other_ref[at, h].astype(F32).reshape(chips // 2 * rows, lanes)
            out_ref[:, h * lanes : (h + 1) * lanes] = jnp.where(first, mine, other)
            out_ref[:, (2 + h) * lanes : (3 + h) * lanes] = jnp.where(first, other, mine)


def lay_weights(mine, other, width):
    return pl.pallas_call(
        weights_kernel,
        out_shape=[jax.ShapeDtypeStruct((width, width), F32)] * 2,
        in_specs=[in_vmem()] * 2,
        out_specs=[in_vmem()] * 2,
        compiler_params=SMALL_PARAMS,
        cost_estimate=cost(width * width, 3 * MIB),
        name="lay_weights",
    )(mine, other)


def body(
    feats,
    stale_feats,
    grad_out,
    stale_bgrad,
    w_self,
    w_neigh,
    adj_tiles,
    tile_source_rows,
    tile_cnt,
    send_idx,
    send_cnt,
):
    peers, slots = send_idx.shape
    nodes, width = feats.shape
    tile_rows = adj_tiles.shape[2]
    all_tiles = (nodes + peers * slots) // tile_rows
    chips = peers // 2
    pairs = [(d, d + 1 - 2 * (d % 2)) for d in range(peers)]
    same_core = [list(range(c, peers, 2)) for c in range(2)]

    def exchange(v, groups):
        return lax.all_to_all(
            v, "dom", split_axis=0, concat_axis=0, tiled=True, axis_index_groups=groups
        )

    slot_rows = send_idx.T
    outgoing = gather(slot_rows, send_cnt, stale_feats)
    incoming = exchange(outgoing, None).reshape(peers * slots, width)
    cb, cbt, cot, self_pre, own_agg, w_self_t, w_neigh_t = combine(
        tile_source_rows, tile_cnt, adj_tiles, feats, w_self, w_neigh, all_tiles
    )
    activated, grad_pre, keep, give = layer(
        cb, incoming, self_pre, own_agg, grad_out, w_neigh, feats, chips
    )
    got = lax.ppermute(give, "dom", pairs)
    parts = exchange(add_pair(keep, got), same_core)
    rows, grad_agg = boundary(cbt, grad_pre, w_neigh_t, peers, slots)
    returned = exchange(lay_shares(parts, rows), None)
    grad_feats = feats_grad(cot, grad_agg, grad_pre, w_self_t, stale_bgrad)
    returned, grad_feats = lax.optimization_barrier((returned, grad_feats))

    mine = take_shares(returned).reshape(keep.shape)
    other = lax.ppermute(mine, "dom", pairs)
    next_bgrad = scatter(slot_rows, send_cnt, returned, nodes)
    grad_w_self, grad_w_neigh = lay_weights(mine, other, width)
    return activated, grad_feats, next_bgrad, grad_w_self, grad_w_neigh


def solution(mesh):
    in_specs = (
        P("dom", None),
        P("dom", None),
        P("dom", None),
        P("dom", None),
        P(),
        P(),
        P("dom", None, None, None),
        P("dom", None),
        P("dom"),
        P("dom", None),
        P("dom", None),
    )
    out_specs = (P("dom", None), P("dom", None), P("dom", None), P(), P())
    return jax.shard_map(body, mesh=mesh, in_specs=in_specs, out_specs=out_specs, check_vma=False)
```

```python
import functools

import jax
import jax.numpy as jnp
from jax import lax
from jax.experimental import pallas as pl
from jax.experimental.pallas import tpu as pltpu
from jax.sharding import PartitionSpec as P

BF16 = jnp.bfloat16
F32 = jnp.float32
LANES = 128
MIB = 1 << 20
GELU_SLOPE = 0.7978845608028654
GELU_CUBIC = 0.044715


def dot(a, b):
    return jnp.dot(a, b, preferred_element_type=F32)


def whole(shape):
    return pl.BlockSpec(shape, lambda *_: (0,) * len(shape))


def scalars():
    return pl.BlockSpec(memory_space=pltpu.SMEM)


def anywhere():
    return pl.BlockSpec(memory_space=pl.ANY)


def in_vmem():
    return pl.BlockSpec(memory_space=pltpu.VMEM)


SMALL_PARAMS = pltpu.CompilerParams(vmem_limit_bytes=16 * MIB)
PARAMS = pltpu.CompilerParams(vmem_limit_bytes=56 * MIB)
LAYER_PARAMS = pltpu.CompilerParams(vmem_limit_bytes=48 * MIB)
BACK_PARAMS = pltpu.CompilerParams(vmem_limit_bytes=56 * MIB)
LAY_PARAMS = pltpu.CompilerParams(vmem_limit_bytes=52 * MIB)


PLANES = 16


def cost(macs, moved):
    return pl.CostEstimate(flops=2 * macs, bytes_accessed=moved, transcendentals=0)


def first_core():
    return lax.rem(lax.axis_index("dom"), 2) == 0


def live_slots(idx_ref, cnt_ref):
    live = lax.broadcasted_iota(jnp.int32, idx_ref.shape, 0) < cnt_ref[...]
    return jnp.where(live, idx_ref[...], -1)


def one_hot(idx, nodes, start, count):
    node_ids = lax.broadcasted_iota(jnp.int32, (idx.shape[0], nodes), 1)
    picks = [
        jnp.where(idx[:, t : t + 1] == node_ids, 1.0, 0.0).astype(BF16)
        for t in range(start, start + count)
    ]
    return jnp.concatenate(picks, axis=0)


def gather_kernel(
    idx_ref, cnt_ref, rows_ref, out_ref, slot_idx, slot_cnt, rows, buf, load_sems, sems
):
    groups = sems.shape[0]
    slots, peers = slot_idx.shape
    nodes, width = rows.shape
    pairs = ((idx_ref, slot_idx), (cnt_ref, slot_cnt), (rows_ref, rows))
    loads = [
        pltpu.make_async_copy(src, dst, load_sems.at[n]) for n, (src, dst) in enumerate(pairs)
    ]
    for load in loads:
        load.start()
    loads[0].wait()
    loads[1].wait()
    idx = live_slots(slot_idx, slot_cnt)
    per = peers // groups
    copies = []
    for g in range(groups):
        picks = one_hot(idx, nodes, g * per, per)
        if g == 0:
            loads[2].wait()
        span = pl.ds(g * per, per)
        buf[span] = dot(picks, rows[...]).astype(BF16).reshape(per, slots, width)
        copy = pltpu.make_async_copy(buf.at[span], out_ref.at[span], sems.at[g])
        copy.start()
        copies.append(copy)
    for copy in copies:
        copy.wait()


def gather(slot_rows, send_cnt, stale_feats, groups=8):
    slots, peers = slot_rows.shape
    nodes, width = stale_feats.shape
    return pl.pallas_call(
        gather_kernel,
        out_shape=jax.ShapeDtypeStruct((peers, slots, width), BF16),
        in_specs=[anywhere()] * 3,
        out_specs=anywhere(),
        scratch_shapes=[
            pltpu.VMEM((slots, peers), jnp.int32),
            pltpu.VMEM((1, peers), jnp.int32),
            pltpu.VMEM((nodes, width), BF16),
            pltpu.VMEM((peers, slots, width), BF16),
            pltpu.SemaphoreType.DMA((3,)),
            pltpu.SemaphoreType.DMA((groups,)),
        ],
        compiler_params=PARAMS,
        cost_estimate=cost(peers * slots * nodes * width, 3 * MIB),
        name="gather_rows",
    )(slot_rows, send_cnt, stale_feats)


def combine_kernel(
    src_ref, cnt_ref, adj_ref, feats_ref, gout_ref, ws_ref, wn_ref,
    cb_ref, cbt_ref, cot_ref, self_ref, own_ref, wst_ref, wnt_ref, late_ref,
    acc,
):
    i = pl.program_id(0)
    tiles, rows = acc.shape[0], acc.shape[1]
    own_tiles = feats_ref.shape[0] // rows
    acc[...] = jnp.zeros_like(acc)

    @pl.when(i == 0)
    def _():
        wst_ref[...] = ws_ref[...].T
        wnt_ref[...] = wn_ref[...].T

    late_ref[0] = gout_ref[...]
    part = lax.rem(i, wn_ref.shape[0] // rows)
    late_ref[1] = wn_ref[pl.ds(pl.multiple_of(part * rows, rows), rows), :]

    @pl.loop(0, cnt_ref[i])
    def _(j):
        s = src_ref[i, j]
        acc[s] += adj_ref[0, j].astype(F32)

    own = []
    for s in range(tiles):
        block = acc[s].astype(BF16)
        if s < own_tiles:
            own.append(block)
            cot_ref[s * rows : (s + 1) * rows, :] = block.T
        else:
            b = s - own_tiles
            cb_ref[:, b * rows : (b + 1) * rows] = block
            cbt_ref[b * rows : (b + 1) * rows, :] = block.T
    feats = feats_ref[...]
    own_ref[...] = dot(jnp.concatenate(own, axis=1), feats)
    mine = feats_ref[pl.ds(pl.multiple_of(i * rows, rows), rows), :]
    self_ref[...] = dot(mine, ws_ref[...])


def combine(tile_source_rows, tile_cnt, adj_tiles, feats, grad_out, w_self, w_neigh, all_tiles):
    dst_tiles, slots, rows, _ = adj_tiles.shape
    nodes, width = feats.shape
    bnd = all_tiles * rows - nodes
    out_shape = [
        jax.ShapeDtypeStruct((nodes, bnd), BF16),
        jax.ShapeDtypeStruct((bnd, nodes), BF16),
        jax.ShapeDtypeStruct((nodes, nodes), BF16),
        jax.ShapeDtypeStruct((nodes, width), F32),
        jax.ShapeDtypeStruct((nodes, width), F32),
        jax.ShapeDtypeStruct((width, width), BF16),
        jax.ShapeDtypeStruct((width, width), BF16),
        jax.ShapeDtypeStruct((PLANES, nodes, width), BF16),
    ]
    return pl.pallas_call(
        combine_kernel,
        grid=(dst_tiles,),
        out_shape=out_shape,
        in_specs=[
            scalars(),
            scalars(),
            pl.BlockSpec((1, slots, rows, rows), lambda i: (i, 0, 0, 0)),
            whole((nodes, width)),
            pl.BlockSpec((rows, width), lambda i: (i, 0)),
            whole((width, width)),
            whole((width, width)),
        ],
        out_specs=[
            pl.BlockSpec((rows, bnd), lambda i: (i, 0)),
            pl.BlockSpec((bnd, rows), lambda i: (0, i)),
            pl.BlockSpec((nodes, rows), lambda i: (0, i)),
            pl.BlockSpec((rows, width), lambda i: (i, 0)),
            pl.BlockSpec((rows, width), lambda i: (i, 0)),
            whole((width, width)),
            whole((width, width)),
            pl.BlockSpec((2, rows, width), lambda i: (0, i, 0)),
        ],
        scratch_shapes=[pltpu.VMEM((all_tiles, rows, rows), F32)],
        compiler_params=PARAMS,
        cost_estimate=cost(nodes * width * (nodes + width), 20 * MIB),
        name="combine_tiles",
    )(tile_source_rows, tile_cnt, adj_tiles, feats, grad_out, w_self, w_neigh)


class Stream:
    def __init__(self, copies, ahead):
        self.copies, self.ahead, self.started = copies, ahead, 0
        self.start(ahead)

    def start(self, count):
        while self.started < min(count, len(self.copies)):
            self.copies[self.started].start()
            self.started += 1

    def wait(self, *copies):
        for copy in copies:
            at = [c is copy for c in self.copies].index(True)
            self.start(at + 1 + self.ahead)
            copy.wait()


def layer_kernel(
    cb_ref, in_ref, self_ref, own_ref, late_ref, feats_ref,
    act_ref, gpre_ref, keep_ref, pass_ref,
    cb, self_pre, own, gout, wn, feats, left, act, gpre, keep, give,
    cb_sems, sems, out_sems,
):
    bnd, width = in_ref.shape
    cuts = [0, bnd // 8, bnd // 4, bnd // 2, 3 * bnd // 4, bnd]
    cuts = list(zip(cuts[:-1], cuts[1:]))
    spans = [pl.ds(a, b - a) for a, b in cuts]
    copy = pltpu.make_async_copy
    get_cb = [copy(cb_ref.at[:, d], cb.at[:, d], cb_sems.at[k]) for k, d in enumerate(spans)]
    rest = [
        (own_ref, own), (late_ref.at[1, pl.ds(0, width)], wn), (self_ref, self_pre),
        (late_ref.at[0], gout),
        (feats_ref, feats),
    ]
    rest = [copy(src, dst, sems.at[n]) for n, (src, dst) in enumerate(rest)]
    loads = Stream(get_cb + rest, 5)
    outs = []

    def put(src, dst):
        outs.append(copy(src, dst, out_sems.at[len(outs)]))
        outs[-1].start()

    total = None
    for k, (a, b) in enumerate(cuts):
        loads.wait(get_cb[k])
        term = dot(cb[:, a:b], in_ref[a:b, :])
        total = term if total is None else total + term
    loads.wait(rest[0])
    agg = (total + own[...]).astype(BF16)
    loads.wait(rest[1], rest[2])
    pre = self_pre[...] + dot(agg, wn[...])
    left[width:, :] = agg.T
    square = pre * pre
    t = jnp.tanh(GELU_SLOPE * pre * (1.0 + GELU_CUBIC * square))
    half = 0.5 * (1.0 + t)
    act[...] = (pre * half).astype(BF16)
    slope = half + 0.5 * pre * (1.0 - t * t) * (
        GELU_SLOPE * (1.0 + (3.0 * GELU_CUBIC) * square)
    )
    loads.wait(rest[3])
    gpre[...] = (gout[...].astype(F32) * slope).astype(BF16)
    put(act, act_ref)
    put(gpre, gpre_ref.at[0])
    loads.wait(rest[4])
    left[:width, :] = feats[...].T
    first = first_core()
    groups, halves, rows, lanes = keep.shape
    g = dot(left[...], gpre[...]).reshape(groups, rows, width)
    for h in range(halves):
        even = g[:, :, 2 * h * lanes : (2 * h + 1) * lanes]
        odd = g[:, :, (2 * h + 1) * lanes : (2 * h + 2) * lanes]
        keep[:, h] = jnp.where(first, even, odd)
        give[:, h] = jnp.where(first, odd, even).astype(BF16)
    put(give, pass_ref)
    put(keep, keep_ref)
    for c in outs:
        c.wait()


def layer(cb, incoming, self_pre, own_agg, late, feats, chips):
    nodes, bnd = cb.shape
    width = incoming.shape[1]
    chunks = 5
    shares = (chips, width // (2 * LANES), 2 * width // chips, LANES)
    vmem = pltpu.VMEM
    sems = pltpu.SemaphoreType.DMA
    return pl.pallas_call(
        layer_kernel,
        out_shape=[
            jax.ShapeDtypeStruct((nodes, width), BF16),
            jax.ShapeDtypeStruct((PLANES, nodes, width), BF16),
            jax.ShapeDtypeStruct(shares, F32),
            jax.ShapeDtypeStruct(shares, BF16),
        ],
        in_specs=[anywhere(), in_vmem()] + [anywhere()] * 4,
        out_specs=[anywhere()] * 4,
        scratch_shapes=[
            vmem((nodes, bnd), BF16),
            vmem((nodes, width), F32),
            vmem((nodes, width), F32),
            vmem((nodes, width), BF16),
            vmem((width, width), BF16),
            vmem((nodes, width), BF16),
            vmem((2 * width, nodes), BF16),
            vmem((nodes, width), BF16),
            vmem((nodes, width), BF16),
            vmem(shares, F32),
            vmem(shares, BF16),
            sems((chunks,)),
            sems((5,)),
            sems((4,)),
        ],
        compiler_params=LAYER_PARAMS,
        cost_estimate=cost(nodes * width * (bnd + 3 * width), 18 * MIB),
        name="layer",
    )(cb, incoming, self_pre, own_agg, late, feats)


def boundary_kernel(
    cbt_ref, gpre_ref, wnt_ref, out_ref, gagg_ref,
    cbt, gpre, wnt, gagg, rows, cbt_sems, sems, out_sems,
):
    chunks = cbt_sems.shape[0]
    peers, slots, width = rows.shape
    nodes = gpre.shape[0]
    per, depth = peers // chunks, cbt.shape[0] // chunks
    copy = pltpu.make_async_copy
    get_w = copy(wnt_ref, wnt, sems.at[0])
    get_gpre = copy(gpre_ref.at[0], gpre, sems.at[1])
    get_cbt = [
        copy(cbt_ref.at[pl.ds(c * depth, depth)], cbt.at[pl.ds(c * depth, depth)], cbt_sems.at[c])
        for c in range(chunks)
    ]
    loads = Stream([get_w, get_gpre] + get_cbt, 3)
    outs = []

    def put(src, dst):
        outs.append(copy(src, dst, out_sems.at[len(outs)]))
        outs[-1].start()

    loads.wait(get_w, get_gpre)
    gagg[...] = dot(gpre[...], wnt[...]).astype(BF16)
    put(gagg, gagg_ref)
    for c in range(chunks):
        loads.wait(get_cbt[c])
        got = dot(cbt[c * depth : (c + 1) * depth, :], gagg[...]).astype(BF16)
        at = pl.ds(c * per, per)
        rows[at] = got.reshape(per, slots, width)
        put(rows.at[at], out_ref.at[at, :, pl.ds(0, width)])
    for c in outs:
        c.wait()


def boundary(cbt, grad_pre, w_neigh_t, peers, slots):
    bnd, nodes = cbt.shape
    width = grad_pre.shape[2]
    chunks = 4
    vmem = pltpu.VMEM
    return pl.pallas_call(
        boundary_kernel,
        out_shape=[
            jax.ShapeDtypeStruct((peers, slots, width + LANES), BF16),
            jax.ShapeDtypeStruct((nodes, width), BF16),
        ],
        in_specs=[anywhere()] * 3,
        out_specs=[anywhere()] * 2,
        scratch_shapes=[
            vmem((bnd, nodes), BF16),
            vmem((nodes, width), BF16),
            vmem((width, width), BF16),
            vmem((nodes, width), BF16),
            vmem((peers, slots, width), BF16),
            pltpu.SemaphoreType.DMA((chunks,)),
            pltpu.SemaphoreType.DMA((2,)),
            pltpu.SemaphoreType.DMA((chunks + 1,)),
        ],
        compiler_params=BACK_PARAMS,
        cost_estimate=cost((bnd + width) * nodes * width, 9 * MIB),
        name="boundary_grads",
    )(cbt, grad_pre, w_neigh_t)


def feats_grad_kernel(cot_ref, gagg_ref, gpre_ref, wst_ref, stale_ref, out_ref):
    total = dot(gpre_ref[0], wst_ref[...]) + dot(cot_ref[...], gagg_ref[...])
    out_ref[...] = (total + stale_ref[...].astype(F32)).astype(BF16)


def feats_grad(cot, grad_agg, grad_pre, w_self_t, stale_bgrad):
    nodes, width = grad_agg.shape
    block = 512
    by_block = lambda w: pl.BlockSpec((block, w), lambda i: (i, 0))
    return pl.pallas_call(
        feats_grad_kernel,
        grid=(nodes // block,),
        out_shape=jax.ShapeDtypeStruct((nodes, width), BF16),
        in_specs=[
            by_block(nodes),
            whole((nodes, width)),
            pl.BlockSpec((1, block, width), lambda i: (0, i, 0)),
            whole((width, width)),
            by_block(width),
        ],
        out_specs=by_block(width),
        compiler_params=PARAMS,
        cost_estimate=cost(nodes * width * (nodes + width), 7 * MIB),
        name="feats_grad",
    )(cot, grad_agg, grad_pre, w_self_t, stale_bgrad)


def add_kernel(keep_ref, got_ref, out_ref):
    out_ref[...] = (keep_ref[...] + got_ref[...].astype(F32)).astype(BF16)


def add_pair(keep, got):
    return pl.pallas_call(
        add_kernel,
        out_shape=jax.ShapeDtypeStruct(keep.shape, BF16),
        in_specs=[in_vmem()] * 2,
        out_specs=in_vmem(),
        compiler_params=SMALL_PARAMS,
        cost_estimate=cost(keep.size, 2 * MIB),
        name="add_pair",
    )(keep, got)


def take_kernel(ret_ref, out_ref):
    out_ref[...] = ret_ref[:, :, ret_ref.shape[2] - LANES :]


def take_shares(returned):
    peers, slots, _ = returned.shape
    return pl.pallas_call(
        take_kernel,
        out_shape=jax.ShapeDtypeStruct((peers, slots, LANES), BF16),
        in_specs=[in_vmem()],
        out_specs=in_vmem(),
        compiler_params=SMALL_PARAMS,
        cost_estimate=cost(peers * slots * LANES, MIB),
        name="take_shares",
    )(returned)


def share_kernel(parts_ref, _, out_ref, buf, sem):
    total = parts_ref[0].astype(F32)
    for c in range(1, parts_ref.shape[0]):
        total += parts_ref[c].astype(F32)
    total = total.astype(BF16)
    for p in range(buf.shape[0]):
        buf[p] = total[p % 2]
    width = out_ref.shape[2] - LANES
    copy = pltpu.make_async_copy(buf, out_ref.at[:, :, pl.ds(width, LANES)], sem)
    copy.start()
    copy.wait()


def lay_shares(parts, rows):
    peers, slots, _ = rows.shape
    return pl.pallas_call(
        share_kernel,
        out_shape=jax.ShapeDtypeStruct(rows.shape, BF16),
        in_specs=[in_vmem(), anywhere()],
        out_specs=anywhere(),
        scratch_shapes=[pltpu.VMEM((peers, slots, LANES), BF16), pltpu.SemaphoreType.DMA],
        input_output_aliases={1: 0},
        compiler_params=LAY_PARAMS,
        cost_estimate=cost(parts.size, MIB),
        name="lay_shares",
    )(parts, rows)


def slots_by_lane(idx, lanes):
    slots, peers = idx.shape
    per = lanes // slots
    tall = jnp.concatenate([idx] * per, axis=0).T
    peer = lax.broadcasted_iota(jnp.int32, tall.shape, 0)
    lane = lax.broadcasted_iota(jnp.int32, tall.shape, 1)
    return jnp.where(peer % per == lane // slots, tall, 0).reshape(peers // per, per, lanes).sum(axis=1)


def scatter_kernel(idx_ref, cnt_ref, ret_ref, out_ref, *, chunks):
    peers, slots, _ = ret_ref.shape
    nodes, width = out_ref.shape
    per = peers // chunks
    idx = slots_by_lane(live_slots(idx_ref, cnt_ref), LANES)
    node_ids = lax.broadcasted_iota(jnp.int32, (nodes, LANES), 0)
    count = per * slots // LANES
    total = None
    for c in range(chunks):
        picks = [
            jnp.where(idx[n : n + 1, :] == node_ids, 1.0, 0.0).astype(BF16)
            for n in range(c * count, (c + 1) * count)
        ]
        rows = ret_ref[c * per : (c + 1) * per, :, :width].reshape(per * slots, width)
        term = dot(jnp.concatenate(picks, axis=1), rows)
        total = term if total is None else total + term
    out_ref[...] = total.astype(BF16)


def scatter(slot_rows, send_cnt, returned, nodes, chunks=4):
    width = returned.shape[2] - LANES
    return pl.pallas_call(
        functools.partial(scatter_kernel, chunks=chunks),
        out_shape=jax.ShapeDtypeStruct((nodes, width), BF16),
        in_specs=[in_vmem()] * 3,
        out_specs=in_vmem(),
        compiler_params=SMALL_PARAMS,
        cost_estimate=cost(returned.size * nodes, 4 * MIB),
        name="scatter_rows",
    )(slot_rows, send_cnt, returned)


def weights_kernel(mine_ref, other_ref, ws_ref, wn_ref):
    first = first_core()
    chips, halves, rows, lanes = mine_ref.shape
    for part, out_ref in enumerate((ws_ref, wn_ref)):
        at = pl.ds(part * (chips // 2), chips // 2)
        for h in range(halves):
            mine = mine_ref[at, h].astype(F32).reshape(chips // 2 * rows, lanes)
            other = other_ref[at, h].astype(F32).reshape(chips // 2 * rows, lanes)
            out_ref[:, h * lanes : (h + 1) * lanes] = jnp.where(first, mine, other)
            out_ref[:, (2 + h) * lanes : (3 + h) * lanes] = jnp.where(first, other, mine)


def lay_weights(mine, other, width):
    return pl.pallas_call(
        weights_kernel,
        out_shape=[jax.ShapeDtypeStruct((width, width), F32)] * 2,
        in_specs=[in_vmem()] * 2,
        out_specs=[in_vmem()] * 2,
        compiler_params=SMALL_PARAMS,
        cost_estimate=cost(width * width, 3 * MIB),
        name="lay_weights",
    )(mine, other)


def body(
    feats,
    stale_feats,
    grad_out,
    stale_bgrad,
    w_self,
    w_neigh,
    adj_tiles,
    tile_source_rows,
    tile_cnt,
    send_idx,
    send_cnt,
):
    peers, slots = send_idx.shape
    nodes, width = feats.shape
    tile_rows = adj_tiles.shape[2]
    all_tiles = (nodes + peers * slots) // tile_rows
    chips = peers // 2
    pairs = [(d, d + 1 - 2 * (d % 2)) for d in range(peers)]
    same_core = [list(range(c, peers, 2)) for c in range(2)]

    def exchange(v, groups):
        return lax.all_to_all(
            v, "dom", split_axis=0, concat_axis=0, tiled=True, axis_index_groups=groups
        )

    slot_rows = send_idx.T
    outgoing = gather(slot_rows, send_cnt, stale_feats)
    incoming = exchange(outgoing, None).reshape(peers * slots, width)
    cb, cbt, cot, self_pre, own_agg, w_self_t, w_neigh_t, late = combine(
        tile_source_rows, tile_cnt, adj_tiles, feats, grad_out, w_self, w_neigh, all_tiles
    )
    activated, grad_pre, keep, give = layer(
        cb, incoming, self_pre, own_agg, late, feats, chips
    )
    got = lax.ppermute(give, "dom", pairs)
    parts = exchange(add_pair(keep, got), same_core)
    rows, grad_agg = boundary(cbt, grad_pre, w_neigh_t, peers, slots)
    returned = exchange(lay_shares(parts, rows), None)
    grad_feats = feats_grad(cot, grad_agg, grad_pre, w_self_t, stale_bgrad)
    returned, grad_feats = lax.optimization_barrier((returned, grad_feats))

    mine = take_shares(returned).reshape(keep.shape)
    other = lax.ppermute(mine, "dom", pairs)
    next_bgrad = scatter(slot_rows, send_cnt, returned, nodes)
    grad_w_self, grad_w_neigh = lay_weights(mine, other, width)
    return activated, grad_feats, next_bgrad, grad_w_self, grad_w_neigh


def solution(mesh):
    in_specs = (
        P("dom", None),
        P("dom", None),
        P("dom", None),
        P("dom", None),
        P(),
        P(),
        P("dom", None, None, None),
        P("dom", None),
        P("dom"),
        P("dom", None),
        P("dom", None),
    )
    out_specs = (P("dom", None), P("dom", None), P("dom", None), P(), P())
    return jax.shard_map(body, mesh=mesh, in_specs=in_specs, out_specs=out_specs, check_vma=False)
```

```python
import functools

import jax
import jax.numpy as jnp
from jax import lax
from jax.experimental import pallas as pl
from jax.experimental.pallas import tpu as pltpu
from jax.sharding import PartitionSpec as P

BF16 = jnp.bfloat16
F32 = jnp.float32
LANES = 128
MIB = 1 << 20
GELU_SLOPE = 0.7978845608028654
GELU_CUBIC = 0.044715


def dot(a, b):
    return jnp.dot(a, b, preferred_element_type=F32)


def whole(shape):
    return pl.BlockSpec(shape, lambda *_: (0,) * len(shape))


def scalars():
    return pl.BlockSpec(memory_space=pltpu.SMEM)


def anywhere():
    return pl.BlockSpec(memory_space=pl.ANY)


def in_vmem():
    return pl.BlockSpec(memory_space=pltpu.VMEM)


SMALL_PARAMS = pltpu.CompilerParams(vmem_limit_bytes=16 * MIB)
PARAMS = pltpu.CompilerParams(vmem_limit_bytes=56 * MIB)
LAYER_PARAMS = pltpu.CompilerParams(vmem_limit_bytes=50 * MIB)
BACK_PARAMS = pltpu.CompilerParams(vmem_limit_bytes=56 * MIB)
LAY_PARAMS = pltpu.CompilerParams(vmem_limit_bytes=52 * MIB)


PLANES = 16


def cost(macs, moved):
    return pl.CostEstimate(flops=2 * macs, bytes_accessed=moved, transcendentals=0)


def first_core():
    return lax.rem(lax.axis_index("dom"), 2) == 0


def live_slots(idx_ref, cnt_ref):
    live = lax.broadcasted_iota(jnp.int32, idx_ref.shape, 0) < cnt_ref[...]
    return jnp.where(live, idx_ref[...], -1)


def one_hot(idx, nodes, start, count):
    node_ids = lax.broadcasted_iota(jnp.int32, (idx.shape[0], nodes), 1)
    picks = [
        jnp.where(idx[:, t : t + 1] == node_ids, 1.0, 0.0).astype(BF16)
        for t in range(start, start + count)
    ]
    return jnp.concatenate(picks, axis=0)


def gather_kernel(
    idx_ref, cnt_ref, rows_ref, out_ref, slot_idx, slot_cnt, rows, buf, load_sems, sems
):
    groups = sems.shape[0]
    slots, peers = slot_idx.shape
    nodes, width = rows.shape
    pairs = ((idx_ref, slot_idx), (cnt_ref, slot_cnt), (rows_ref, rows))
    loads = [
        pltpu.make_async_copy(src, dst, load_sems.at[n]) for n, (src, dst) in enumerate(pairs)
    ]
    for load in loads:
        load.start()
    loads[0].wait()
    loads[1].wait()
    idx = live_slots(slot_idx, slot_cnt)
    per = peers // groups
    copies = []
    for g in range(groups):
        picks = one_hot(idx, nodes, g * per, per)
        if g == 0:
            loads[2].wait()
        span = pl.ds(g * per, per)
        buf[span] = dot(picks, rows[...]).astype(BF16).reshape(per, slots, width)
        copy = pltpu.make_async_copy(buf.at[span], out_ref.at[span], sems.at[g])
        copy.start()
        copies.append(copy)
    for copy in copies:
        copy.wait()


def gather(slot_rows, send_cnt, stale_feats, groups=8):
    slots, peers = slot_rows.shape
    nodes, width = stale_feats.shape
    return pl.pallas_call(
        gather_kernel,
        out_shape=jax.ShapeDtypeStruct((peers, slots, width), BF16),
        in_specs=[anywhere()] * 3,
        out_specs=anywhere(),
        scratch_shapes=[
            pltpu.VMEM((slots, peers), jnp.int32),
            pltpu.VMEM((1, peers), jnp.int32),
            pltpu.VMEM((nodes, width), BF16),
            pltpu.VMEM((peers, slots, width), BF16),
            pltpu.SemaphoreType.DMA((3,)),
            pltpu.SemaphoreType.DMA((groups,)),
        ],
        compiler_params=PARAMS,
        cost_estimate=cost(peers * slots * nodes * width, 3 * MIB),
        name="gather_rows",
    )(slot_rows, send_cnt, stale_feats)


def combine_kernel(
    src_ref, cnt_ref, adj_ref, feats_ref, gout_ref, ws_ref, wn_ref,
    cb_ref, cbt_ref, cot_ref, self_ref, own_ref, wst_ref, wnt_ref, late_ref, ft_ref,
    acc,
):
    i = pl.program_id(0)
    tiles, rows = acc.shape[0], acc.shape[1]
    own_tiles = feats_ref.shape[0] // rows
    acc[...] = jnp.zeros_like(acc)

    @pl.when(i == 0)
    def _():
        wst_ref[...] = ws_ref[...].T
        wnt_ref[...] = wn_ref[...].T

    late_ref[0] = gout_ref[...]
    part = lax.rem(i, wn_ref.shape[0] // rows)
    late_ref[1] = wn_ref[pl.ds(pl.multiple_of(part * rows, rows), rows), :]

    @pl.loop(0, cnt_ref[i])
    def _(j):
        s = src_ref[i, j]
        acc[s] += adj_ref[0, j].astype(F32)

    own = []
    for s in range(tiles):
        block = acc[s].astype(BF16)
        if s < own_tiles:
            own.append(block)
            cot_ref[s * rows : (s + 1) * rows, :] = block.T
        else:
            b = s - own_tiles
            cb_ref[:, b * rows : (b + 1) * rows] = block
            cbt_ref[b * rows : (b + 1) * rows, :] = block.T
    feats = feats_ref[...]
    own_ref[...] = dot(jnp.concatenate(own, axis=1), feats)
    mine = feats_ref[pl.ds(pl.multiple_of(i * rows, rows), rows), :]
    self_ref[...] = dot(mine, ws_ref[...])
    ft_ref[0] = mine.T


def combine(tile_source_rows, tile_cnt, adj_tiles, feats, grad_out, w_self, w_neigh, all_tiles):
    dst_tiles, slots, rows, _ = adj_tiles.shape
    nodes, width = feats.shape
    bnd = all_tiles * rows - nodes
    out_shape = [
        jax.ShapeDtypeStruct((nodes, bnd), BF16),
        jax.ShapeDtypeStruct((bnd, nodes), BF16),
        jax.ShapeDtypeStruct((nodes, nodes), BF16),
        jax.ShapeDtypeStruct((nodes, width), F32),
        jax.ShapeDtypeStruct((nodes, width), F32),
        jax.ShapeDtypeStruct((width, width), BF16),
        jax.ShapeDtypeStruct((width, width), BF16),
        jax.ShapeDtypeStruct((PLANES, nodes, width), BF16),
        jax.ShapeDtypeStruct((PLANES, width, nodes), BF16),
    ]
    return pl.pallas_call(
        combine_kernel,
        grid=(dst_tiles,),
        out_shape=out_shape,
        in_specs=[
            scalars(),
            scalars(),
            pl.BlockSpec((1, slots, rows, rows), lambda i: (i, 0, 0, 0)),
            whole((nodes, width)),
            pl.BlockSpec((rows, width), lambda i: (i, 0)),
            whole((width, width)),
            whole((width, width)),
        ],
        out_specs=[
            pl.BlockSpec((rows, bnd), lambda i: (i, 0)),
            pl.BlockSpec((bnd, rows), lambda i: (0, i)),
            pl.BlockSpec((nodes, rows), lambda i: (0, i)),
            pl.BlockSpec((rows, width), lambda i: (i, 0)),
            pl.BlockSpec((rows, width), lambda i: (i, 0)),
            whole((width, width)),
            whole((width, width)),
            pl.BlockSpec((2, rows, width), lambda i: (0, i, 0)),
            pl.BlockSpec((1, width, rows), lambda i: (0, 0, i)),
        ],
        scratch_shapes=[pltpu.VMEM((all_tiles, rows, rows), F32)],
        compiler_params=PARAMS,
        cost_estimate=cost(nodes * width * (nodes + width), 20 * MIB),
        name="combine_tiles",
    )(tile_source_rows, tile_cnt, adj_tiles, feats, grad_out, w_self, w_neigh)


class Stream:
    def __init__(self, copies, ahead):
        self.copies, self.ahead, self.started = copies, ahead, 0
        self.start(ahead)

    def start(self, count):
        while self.started < min(count, len(self.copies)):
            self.copies[self.started].start()
            self.started += 1

    def wait(self, *copies):
        for copy in copies:
            at = [c is copy for c in self.copies].index(True)
            self.start(at + 1 + self.ahead)
            copy.wait()


def layer_kernel(
    cb_ref, in_ref, self_ref, own_ref, late_ref, ft_ref,
    act_ref, gpre_ref, keep_ref, pass_ref,
    cb, self_pre, own, gout, wn, left, act, gpre, keep, give,
    cb_sems, sems, out_sems,
):
    bnd, width = in_ref.shape
    cuts = [0, bnd // 8, bnd // 4, bnd // 2, 3 * bnd // 4, bnd]
    cuts = list(zip(cuts[:-1], cuts[1:]))
    spans = [pl.ds(a, b - a) for a, b in cuts]
    copy = pltpu.make_async_copy
    get_cb = [copy(cb_ref.at[:, d], cb.at[:, d], cb_sems.at[k]) for k, d in enumerate(spans)]
    rest = [
        (own_ref, own), (late_ref.at[1, pl.ds(0, width)], wn), (self_ref, self_pre),
        (late_ref.at[0], gout),
        (ft_ref.at[0], left.at[pl.ds(0, width)]),
    ]
    rest = [copy(src, dst, sems.at[n]) for n, (src, dst) in enumerate(rest)]
    loads = Stream(get_cb + rest, 5)
    outs = []

    def put(src, dst):
        outs.append(copy(src, dst, out_sems.at[len(outs)]))
        outs[-1].start()

    total = None
    for k, (a, b) in enumerate(cuts):
        loads.wait(get_cb[k])
        term = dot(cb[:, a:b], in_ref[a:b, :])
        total = term if total is None else total + term
    loads.wait(rest[0])
    agg = (total + own[...]).astype(BF16)
    loads.wait(rest[1], rest[2])
    pre = self_pre[...] + dot(agg, wn[...])
    left[width:, :] = agg.T
    square = pre * pre
    t = jnp.tanh(GELU_SLOPE * pre * (1.0 + GELU_CUBIC * square))
    half = 0.5 * (1.0 + t)
    act[...] = (pre * half).astype(BF16)
    slope = half + 0.5 * pre * (1.0 - t * t) * (
        GELU_SLOPE * (1.0 + (3.0 * GELU_CUBIC) * square)
    )
    loads.wait(rest[3])
    gpre[...] = (gout[...].astype(F32) * slope).astype(BF16)
    put(act, act_ref)
    put(gpre, gpre_ref.at[0])
    loads.wait(rest[4])
    first = first_core()
    groups, halves, rows, lanes = keep.shape
    g = dot(left[...], gpre[...]).reshape(groups, rows, width)
    for h in range(halves):
        even = g[:, :, 2 * h * lanes : (2 * h + 1) * lanes]
        odd = g[:, :, (2 * h + 1) * lanes : (2 * h + 2) * lanes]
        keep[:, h] = jnp.where(first, even, odd)
        give[:, h] = jnp.where(first, odd, even).astype(BF16)
    put(give, pass_ref)
    put(keep, keep_ref)
    for c in outs:
        c.wait()


def layer(cb, incoming, self_pre, own_agg, late, feats_t, chips):
    nodes, bnd = cb.shape
    width = incoming.shape[1]
    chunks = 5
    shares = (chips, width // (2 * LANES), 2 * width // chips, LANES)
    vmem = pltpu.VMEM
    sems = pltpu.SemaphoreType.DMA
    return pl.pallas_call(
        layer_kernel,
        out_shape=[
            jax.ShapeDtypeStruct((nodes, width), BF16),
            jax.ShapeDtypeStruct((PLANES, nodes, width), BF16),
            jax.ShapeDtypeStruct(shares, F32),
            jax.ShapeDtypeStruct(shares, BF16),
        ],
        in_specs=[anywhere(), in_vmem()] + [anywhere()] * 4,
        out_specs=[anywhere()] * 4,
        scratch_shapes=[
            vmem((nodes, bnd), BF16),
            vmem((nodes, width), F32),
            vmem((nodes, width), F32),
            vmem((nodes, width), BF16),
            vmem((width, width), BF16),
            vmem((2 * width, nodes), BF16),
            vmem((nodes, width), BF16),
            vmem((nodes, width), BF16),
            vmem(shares, F32),
            vmem(shares, BF16),
            sems((chunks,)),
            sems((5,)),
            sems((4,)),
        ],
        compiler_params=LAYER_PARAMS,
        cost_estimate=cost(nodes * width * (bnd + 3 * width), 18 * MIB),
        name="layer",
    )(cb, incoming, self_pre, own_agg, late, feats_t)


def boundary_kernel(
    cbt_ref, gpre_ref, wnt_ref, out_ref, gagg_ref,
    cbt, gpre, wnt, gagg, rows, cbt_sems, sems, out_sems,
):
    chunks = cbt_sems.shape[0]
    peers, slots, width = rows.shape
    nodes = gpre.shape[0]
    per, depth = peers // chunks, cbt.shape[0] // chunks
    copy = pltpu.make_async_copy
    get_w = copy(wnt_ref, wnt, sems.at[0])
    get_gpre = copy(gpre_ref.at[0], gpre, sems.at[1])
    get_cbt = [
        copy(cbt_ref.at[pl.ds(c * depth, depth)], cbt.at[pl.ds(c * depth, depth)], cbt_sems.at[c])
        for c in range(chunks)
    ]
    loads = Stream([get_w, get_gpre] + get_cbt, 3)
    outs = []

    def put(src, dst):
        outs.append(copy(src, dst, out_sems.at[len(outs)]))
        outs[-1].start()

    loads.wait(get_w, get_gpre)
    gagg[...] = dot(gpre[...], wnt[...]).astype(BF16)
    put(gagg, gagg_ref)
    for c in range(chunks):
        loads.wait(get_cbt[c])
        got = dot(cbt[c * depth : (c + 1) * depth, :], gagg[...]).astype(BF16)
        at = pl.ds(c * per, per)
        rows[at] = got.reshape(per, slots, width)
        put(rows.at[at], out_ref.at[at, :, pl.ds(0, width)])
    for c in outs:
        c.wait()


def boundary(cbt, grad_pre, w_neigh_t, peers, slots):
    bnd, nodes = cbt.shape
    width = grad_pre.shape[2]
    chunks = 4
    vmem = pltpu.VMEM
    return pl.pallas_call(
        boundary_kernel,
        out_shape=[
            jax.ShapeDtypeStruct((peers, slots, width + LANES), BF16),
            jax.ShapeDtypeStruct((nodes, width), BF16),
        ],
        in_specs=[anywhere()] * 3,
        out_specs=[anywhere()] * 2,
        scratch_shapes=[
            vmem((bnd, nodes), BF16),
            vmem((nodes, width), BF16),
            vmem((width, width), BF16),
            vmem((nodes, width), BF16),
            vmem((peers, slots, width), BF16),
            pltpu.SemaphoreType.DMA((chunks,)),
            pltpu.SemaphoreType.DMA((2,)),
            pltpu.SemaphoreType.DMA((chunks + 1,)),
        ],
        compiler_params=BACK_PARAMS,
        cost_estimate=cost((bnd + width) * nodes * width, 9 * MIB),
        name="boundary_grads",
    )(cbt, grad_pre, w_neigh_t)


def feats_grad_kernel(cot_ref, gagg_ref, gpre_ref, wst_ref, stale_ref, out_ref):
    total = dot(gpre_ref[0], wst_ref[...]) + dot(cot_ref[...], gagg_ref[...])
    out_ref[...] = (total + stale_ref[...].astype(F32)).astype(BF16)


def feats_grad(cot, grad_agg, grad_pre, w_self_t, stale_bgrad):
    nodes, width = grad_agg.shape
    block = 512
    by_block = lambda w: pl.BlockSpec((block, w), lambda i: (i, 0))
    return pl.pallas_call(
        feats_grad_kernel,
        grid=(nodes // block,),
        out_shape=jax.ShapeDtypeStruct((nodes, width), BF16),
        in_specs=[
            by_block(nodes),
            whole((nodes, width)),
            pl.BlockSpec((1, block, width), lambda i: (0, i, 0)),
            whole((width, width)),
            by_block(width),
        ],
        out_specs=by_block(width),
        compiler_params=PARAMS,
        cost_estimate=cost(nodes * width * (nodes + width), 7 * MIB),
        name="feats_grad",
    )(cot, grad_agg, grad_pre, w_self_t, stale_bgrad)


def add_kernel(keep_ref, got_ref, out_ref):
    out_ref[...] = (keep_ref[...] + got_ref[...].astype(F32)).astype(BF16)


def add_pair(keep, got):
    return pl.pallas_call(
        add_kernel,
        out_shape=jax.ShapeDtypeStruct(keep.shape, BF16),
        in_specs=[in_vmem()] * 2,
        out_specs=in_vmem(),
        compiler_params=SMALL_PARAMS,
        cost_estimate=cost(keep.size, 2 * MIB),
        name="add_pair",
    )(keep, got)


def take_kernel(ret_ref, out_ref):
    out_ref[...] = ret_ref[:, :, ret_ref.shape[2] - LANES :]


def take_shares(returned):
    peers, slots, _ = returned.shape
    return pl.pallas_call(
        take_kernel,
        out_shape=jax.ShapeDtypeStruct((peers, slots, LANES), BF16),
        in_specs=[in_vmem()],
        out_specs=in_vmem(),
        compiler_params=SMALL_PARAMS,
        cost_estimate=cost(peers * slots * LANES, MIB),
        name="take_shares",
    )(returned)


def share_kernel(parts_ref, _, out_ref, buf, sem):
    total = parts_ref[0].astype(F32)
    for c in range(1, parts_ref.shape[0]):
        total += parts_ref[c].astype(F32)
    total = total.astype(BF16)
    for p in range(buf.shape[0]):
        buf[p] = total[p % 2]
    width = out_ref.shape[2] - LANES
    copy = pltpu.make_async_copy(buf, out_ref.at[:, :, pl.ds(width, LANES)], sem)
    copy.start()
    copy.wait()


def lay_shares(parts, rows):
    peers, slots, _ = rows.shape
    return pl.pallas_call(
        share_kernel,
        out_shape=jax.ShapeDtypeStruct(rows.shape, BF16),
        in_specs=[in_vmem(), anywhere()],
        out_specs=anywhere(),
        scratch_shapes=[pltpu.VMEM((peers, slots, LANES), BF16), pltpu.SemaphoreType.DMA],
        input_output_aliases={1: 0},
        compiler_params=LAY_PARAMS,
        cost_estimate=cost(parts.size, MIB),
        name="lay_shares",
    )(parts, rows)


def slots_by_lane(idx, lanes):
    slots, peers = idx.shape
    per = lanes // slots
    tall = jnp.concatenate([idx] * per, axis=0).T
    peer = lax.broadcasted_iota(jnp.int32, tall.shape, 0)
    lane = lax.broadcasted_iota(jnp.int32, tall.shape, 1)
    return jnp.where(peer % per == lane // slots, tall, 0).reshape(peers // per, per, lanes).sum(axis=1)


def scatter_kernel(idx_ref, cnt_ref, ret_ref, out_ref, *, chunks):
    peers, slots, _ = ret_ref.shape
    nodes, width = out_ref.shape
    per = peers // chunks
    idx = slots_by_lane(live_slots(idx_ref, cnt_ref), LANES)
    node_ids = lax.broadcasted_iota(jnp.int32, (nodes, LANES), 0)
    count = per * slots // LANES
    total = None
    for c in range(chunks):
        picks = [
            jnp.where(idx[n : n + 1, :] == node_ids, 1.0, 0.0).astype(BF16)
            for n in range(c * count, (c + 1) * count)
        ]
        rows = ret_ref[c * per : (c + 1) * per, :, :width].reshape(per * slots, width)
        term = dot(jnp.concatenate(picks, axis=1), rows)
        total = term if total is None else total + term
    out_ref[...] = total.astype(BF16)


def scatter(slot_rows, send_cnt, returned, nodes, chunks=4):
    width = returned.shape[2] - LANES
    return pl.pallas_call(
        functools.partial(scatter_kernel, chunks=chunks),
        out_shape=jax.ShapeDtypeStruct((nodes, width), BF16),
        in_specs=[in_vmem()] * 3,
        out_specs=in_vmem(),
        compiler_params=SMALL_PARAMS,
        cost_estimate=cost(returned.size * nodes, 4 * MIB),
        name="scatter_rows",
    )(slot_rows, send_cnt, returned)


def weights_kernel(mine_ref, other_ref, ws_ref, wn_ref):
    first = first_core()
    chips, halves, rows, lanes = mine_ref.shape
    for part, out_ref in enumerate((ws_ref, wn_ref)):
        at = pl.ds(part * (chips // 2), chips // 2)
        for h in range(halves):
            mine = mine_ref[at, h].astype(F32).reshape(chips // 2 * rows, lanes)
            other = other_ref[at, h].astype(F32).reshape(chips // 2 * rows, lanes)
            out_ref[:, h * lanes : (h + 1) * lanes] = jnp.where(first, mine, other)
            out_ref[:, (2 + h) * lanes : (3 + h) * lanes] = jnp.where(first, other, mine)


def lay_weights(mine, other, width):
    return pl.pallas_call(
        weights_kernel,
        out_shape=[jax.ShapeDtypeStruct((width, width), F32)] * 2,
        in_specs=[in_vmem()] * 2,
        out_specs=[in_vmem()] * 2,
        compiler_params=SMALL_PARAMS,
        cost_estimate=cost(width * width, 3 * MIB),
        name="lay_weights",
    )(mine, other)


def body(
    feats,
    stale_feats,
    grad_out,
    stale_bgrad,
    w_self,
    w_neigh,
    adj_tiles,
    tile_source_rows,
    tile_cnt,
    send_idx,
    send_cnt,
):
    peers, slots = send_idx.shape
    nodes, width = feats.shape
    tile_rows = adj_tiles.shape[2]
    all_tiles = (nodes + peers * slots) // tile_rows
    chips = peers // 2
    pairs = [(d, d + 1 - 2 * (d % 2)) for d in range(peers)]
    same_core = [list(range(c, peers, 2)) for c in range(2)]

    def exchange(v, groups):
        return lax.all_to_all(
            v, "dom", split_axis=0, concat_axis=0, tiled=True, axis_index_groups=groups
        )

    slot_rows = send_idx.T
    outgoing = gather(slot_rows, send_cnt, stale_feats)
    incoming = exchange(outgoing, None).reshape(peers * slots, width)
    cb, cbt, cot, self_pre, own_agg, w_self_t, w_neigh_t, late, feats_t = combine(
        tile_source_rows, tile_cnt, adj_tiles, feats, grad_out, w_self, w_neigh, all_tiles
    )
    activated, grad_pre, keep, give = layer(
        cb, incoming, self_pre, own_agg, late, feats_t, chips
    )
    got = lax.ppermute(give, "dom", pairs)
    parts = exchange(add_pair(keep, got), same_core)
    rows, grad_agg = boundary(cbt, grad_pre, w_neigh_t, peers, slots)
    returned = exchange(lay_shares(parts, rows), None)
    grad_feats = feats_grad(cot, grad_agg, grad_pre, w_self_t, stale_bgrad)
    returned, grad_feats = lax.optimization_barrier((returned, grad_feats))

    mine = take_shares(returned).reshape(keep.shape)
    other = lax.ppermute(mine, "dom", pairs)
    next_bgrad = scatter(slot_rows, send_cnt, returned, nodes)
    grad_w_self, grad_w_neigh = lay_weights(mine, other, width)
    return activated, grad_feats, next_bgrad, grad_w_self, grad_w_neigh


def solution(mesh):
    in_specs = (
        P("dom", None),
        P("dom", None),
        P("dom", None),
        P("dom", None),
        P(),
        P(),
        P("dom", None, None, None),
        P("dom", None),
        P("dom"),
        P("dom", None),
        P("dom", None),
    )
    out_specs = (P("dom", None), P("dom", None), P("dom", None), P(), P())
    return jax.shard_map(body, mesh=mesh, in_specs=in_specs, out_specs=out_specs, check_vma=False)
```

```python
import functools

import jax
import jax.numpy as jnp
from jax import lax
from jax.experimental import pallas as pl
from jax.experimental.pallas import tpu as pltpu
from jax.sharding import PartitionSpec as P

BF16 = jnp.bfloat16
F32 = jnp.float32
LANES = 128
MIB = 1 << 20
GELU_SLOPE = 0.7978845608028654
GELU_CUBIC = 0.044715


def dot(a, b):
    return jnp.dot(a, b, preferred_element_type=F32)


def whole(shape):
    return pl.BlockSpec(shape, lambda *_: (0,) * len(shape))


def scalars():
    return pl.BlockSpec(memory_space=pltpu.SMEM)


def anywhere():
    return pl.BlockSpec(memory_space=pl.ANY)


def in_vmem():
    return pl.BlockSpec(memory_space=pltpu.VMEM)


SMALL_PARAMS = pltpu.CompilerParams(vmem_limit_bytes=16 * MIB)
PARAMS = pltpu.CompilerParams(vmem_limit_bytes=56 * MIB)
LAYER_PARAMS = pltpu.CompilerParams(vmem_limit_bytes=50 * MIB)
BACK_PARAMS = pltpu.CompilerParams(vmem_limit_bytes=56 * MIB)
LAY_PARAMS = pltpu.CompilerParams(vmem_limit_bytes=52 * MIB)


PLANES = 16


def cost(macs, moved):
    return pl.CostEstimate(flops=2 * macs, bytes_accessed=moved, transcendentals=0)


def first_core():
    return lax.rem(lax.axis_index("dom"), 2) == 0


def live_slots(idx_ref, cnt_ref):
    live = lax.broadcasted_iota(jnp.int32, idx_ref.shape, 0) < cnt_ref[...]
    return jnp.where(live, idx_ref[...], -1)


def one_hot(idx, nodes, start, count):
    node_ids = lax.broadcasted_iota(jnp.int32, (idx.shape[0], nodes), 1)
    picks = [
        jnp.where(idx[:, t : t + 1] == node_ids, 1.0, 0.0).astype(BF16)
        for t in range(start, start + count)
    ]
    return jnp.concatenate(picks, axis=0)


def gather_kernel(
    idx_ref, cnt_ref, rows_ref, out_ref, slot_idx, slot_cnt, rows, buf, load_sems, sems
):
    groups = sems.shape[0]
    slots, peers = slot_idx.shape
    nodes, width = rows.shape
    pairs = ((idx_ref, slot_idx), (cnt_ref, slot_cnt), (rows_ref, rows))
    loads = [
        pltpu.make_async_copy(src, dst, load_sems.at[n]) for n, (src, dst) in enumerate(pairs)
    ]
    for load in loads:
        load.start()
    loads[0].wait()
    loads[1].wait()
    idx = live_slots(slot_idx, slot_cnt)
    per = peers // groups
    copies = []
    for g in range(groups):
        picks = one_hot(idx, nodes, g * per, per)
        if g == 0:
            loads[2].wait()
        span = pl.ds(g * per, per)
        buf[span] = dot(picks, rows[...]).astype(BF16).reshape(per, slots, width)
        copy = pltpu.make_async_copy(buf.at[span], out_ref.at[span], sems.at[g])
        copy.start()
        copies.append(copy)
    for copy in copies:
        copy.wait()


def gather(slot_rows, send_cnt, stale_feats, groups=8):
    slots, peers = slot_rows.shape
    nodes, width = stale_feats.shape
    return pl.pallas_call(
        gather_kernel,
        out_shape=jax.ShapeDtypeStruct((peers, slots, width), BF16),
        in_specs=[anywhere()] * 3,
        out_specs=anywhere(),
        scratch_shapes=[
            pltpu.VMEM((slots, peers), jnp.int32),
            pltpu.VMEM((1, peers), jnp.int32),
            pltpu.VMEM((nodes, width), BF16),
            pltpu.VMEM((peers, slots, width), BF16),
            pltpu.SemaphoreType.DMA((3,)),
            pltpu.SemaphoreType.DMA((groups,)),
        ],
        compiler_params=PARAMS,
        cost_estimate=cost(peers * slots * nodes * width, 3 * MIB),
        name="gather_rows",
    )(slot_rows, send_cnt, stale_feats)


def combine_kernel(
    src_ref, cnt_ref, adj_ref, feats_ref, gout_ref, ws_ref, wn_ref,
    cb_ref, cbt_ref, cot_ref, self_ref, own_ref, wst_ref, wnt_ref, late_ref, ft_ref,
    acc,
):
    i = pl.program_id(0)
    tiles, rows = acc.shape[0], acc.shape[1]
    own_tiles = feats_ref.shape[0] // rows
    acc[...] = jnp.zeros_like(acc)

    @pl.when(i == 0)
    def _():
        wst_ref[...] = ws_ref[...].T
        wnt_ref[...] = wn_ref[...].T

    late_ref[0] = gout_ref[...]
    part = lax.rem(i, wn_ref.shape[0] // rows)
    late_ref[1] = wn_ref[pl.ds(pl.multiple_of(part * rows, rows), rows), :]

    @pl.loop(0, cnt_ref[i])
    def _(j):
        s = src_ref[i, j]
        acc[s] += adj_ref[0, j].astype(F32)

    own = []
    for s in range(tiles):
        block = acc[s].astype(BF16)
        if s < own_tiles:
            own.append(block)
            cot_ref[s * rows : (s + 1) * rows, :] = block.T
        else:
            b = s - own_tiles
            cb_ref[:, b * rows : (b + 1) * rows] = block
            cbt_ref[b * rows : (b + 1) * rows, :] = block.T
    feats = feats_ref[...]
    own_ref[...] = dot(jnp.concatenate(own, axis=1), feats)
    mine = feats_ref[pl.ds(pl.multiple_of(i * rows, rows), rows), :]
    self_ref[...] = dot(mine, ws_ref[...])
    ft_ref[0] = mine.T


def combine(tile_source_rows, tile_cnt, adj_tiles, feats, grad_out, w_self, w_neigh, all_tiles):
    dst_tiles, slots, rows, _ = adj_tiles.shape
    nodes, width = feats.shape
    bnd = all_tiles * rows - nodes
    out_shape = [
        jax.ShapeDtypeStruct((nodes, bnd), BF16),
        jax.ShapeDtypeStruct((bnd, nodes), BF16),
        jax.ShapeDtypeStruct((nodes, nodes), BF16),
        jax.ShapeDtypeStruct((nodes, width), F32),
        jax.ShapeDtypeStruct((nodes, width), F32),
        jax.ShapeDtypeStruct((width, width), BF16),
        jax.ShapeDtypeStruct((width, width), BF16),
        jax.ShapeDtypeStruct((PLANES, nodes, width), BF16),
        jax.ShapeDtypeStruct((PLANES, width, nodes), BF16),
    ]
    return pl.pallas_call(
        combine_kernel,
        grid=(dst_tiles,),
        out_shape=out_shape,
        in_specs=[
            scalars(),
            scalars(),
            pl.BlockSpec((1, slots, rows, rows), lambda i: (i, 0, 0, 0)),
            whole((nodes, width)),
            pl.BlockSpec((rows, width), lambda i: (i, 0)),
            whole((width, width)),
            whole((width, width)),
        ],
        out_specs=[
            pl.BlockSpec((rows, bnd), lambda i: (i, 0)),
            pl.BlockSpec((bnd, rows), lambda i: (0, i)),
            pl.BlockSpec((nodes, rows), lambda i: (0, i)),
            pl.BlockSpec((rows, width), lambda i: (i, 0)),
            pl.BlockSpec((rows, width), lambda i: (i, 0)),
            whole((width, width)),
            whole((width, width)),
            pl.BlockSpec((2, rows, width), lambda i: (0, i, 0)),
            pl.BlockSpec((1, width, rows), lambda i: (0, 0, i)),
        ],
        scratch_shapes=[pltpu.VMEM((all_tiles, rows, rows), F32)],
        compiler_params=PARAMS,
        cost_estimate=cost(nodes * width * (nodes + width), 20 * MIB),
        name="combine_tiles",
    )(tile_source_rows, tile_cnt, adj_tiles, feats, grad_out, w_self, w_neigh)


class Stream:
    def __init__(self, copies, ahead):
        self.copies, self.ahead, self.started = copies, ahead, 0
        self.start(ahead)

    def start(self, count):
        while self.started < min(count, len(self.copies)):
            self.copies[self.started].start()
            self.started += 1

    def wait(self, *copies):
        for copy in copies:
            at = [c is copy for c in self.copies].index(True)
            self.start(at + 1 + self.ahead)
            copy.wait()


def layer_kernel(
    cb_ref, in_ref, self_ref, own_ref, late_ref, ft_ref,
    act_ref, gpre_ref, keep_ref, pass_ref,
    cb, self_pre, own, gout, wn, left, act, gpre, keep, give,
    cb_sems, sems, out_sems,
):
    bnd, width = in_ref.shape
    cuts = [0, bnd // 8, bnd // 4, bnd // 2, 3 * bnd // 4, bnd]
    cuts = list(zip(cuts[:-1], cuts[1:]))
    spans = [pl.ds(a, b - a) for a, b in cuts]
    copy = pltpu.make_async_copy
    get_cb = [copy(cb_ref.at[:, d], cb.at[:, d], cb_sems.at[k]) for k, d in enumerate(spans)]
    rest = [
        (own_ref, own), (late_ref.at[1, pl.ds(0, width)], wn), (self_ref, self_pre),
        (late_ref.at[0], gout),
        (ft_ref.at[0], left.at[pl.ds(0, width)]),
    ]
    rest = [copy(src, dst, sems.at[n]) for n, (src, dst) in enumerate(rest)]
    loads = Stream(get_cb + rest, 8)
    outs = []

    def put(src, dst):
        outs.append(copy(src, dst, out_sems.at[len(outs)]))
        outs[-1].start()

    total = None
    for k, (a, b) in enumerate(cuts):
        loads.wait(get_cb[k])
        term = dot(cb[:, a:b], in_ref[a:b, :])
        total = term if total is None else total + term
    loads.wait(rest[0])
    agg = (total + own[...]).astype(BF16)
    loads.wait(rest[1], rest[2])
    pre = self_pre[...] + dot(agg, wn[...])
    left[width:, :] = agg.T
    square = pre * pre
    t = jnp.tanh(GELU_SLOPE * pre * (1.0 + GELU_CUBIC * square))
    half = 0.5 * (1.0 + t)
    act[...] = (pre * half).astype(BF16)
    slope = half + 0.5 * pre * (1.0 - t * t) * (
        GELU_SLOPE * (1.0 + (3.0 * GELU_CUBIC) * square)
    )
    loads.wait(rest[3])
    gpre[...] = (gout[...].astype(F32) * slope).astype(BF16)
    put(act, act_ref)
    put(gpre, gpre_ref.at[0])
    loads.wait(rest[4])
    first = first_core()
    groups, halves, rows, lanes = keep.shape
    g = dot(left[...], gpre[...]).reshape(groups, rows, width)
    for h in range(halves):
        even = g[:, :, 2 * h * lanes : (2 * h + 1) * lanes]
        odd = g[:, :, (2 * h + 1) * lanes : (2 * h + 2) * lanes]
        keep[:, h] = jnp.where(first, even, odd)
        give[:, h] = jnp.where(first, odd, even).astype(BF16)
    put(give, pass_ref)
    put(keep, keep_ref)
    for c in outs:
        c.wait()


def layer(cb, incoming, self_pre, own_agg, late, feats_t, chips):
    nodes, bnd = cb.shape
    width = incoming.shape[1]
    chunks = 5
    shares = (chips, width // (2 * LANES), 2 * width // chips, LANES)
    vmem = pltpu.VMEM
    sems = pltpu.SemaphoreType.DMA
    return pl.pallas_call(
        layer_kernel,
        out_shape=[
            jax.ShapeDtypeStruct((nodes, width), BF16),
            jax.ShapeDtypeStruct((PLANES, nodes, width), BF16),
            jax.ShapeDtypeStruct(shares, F32),
            jax.ShapeDtypeStruct(shares, BF16),
        ],
        in_specs=[anywhere(), in_vmem()] + [anywhere()] * 4,
        out_specs=[anywhere()] * 4,
        scratch_shapes=[
            vmem((nodes, bnd), BF16),
            vmem((nodes, width), F32),
            vmem((nodes, width), F32),
            vmem((nodes, width), BF16),
            vmem((width, width), BF16),
            vmem((2 * width, nodes), BF16),
            vmem((nodes, width), BF16),
            vmem((nodes, width), BF16),
            vmem(shares, F32),
            vmem(shares, BF16),
            sems((chunks,)),
            sems((5,)),
            sems((4,)),
        ],
        compiler_params=LAYER_PARAMS,
        cost_estimate=cost(nodes * width * (bnd + 3 * width), 18 * MIB),
        name="layer",
    )(cb, incoming, self_pre, own_agg, late, feats_t)


def boundary_kernel(
    cbt_ref, gpre_ref, wnt_ref, out_ref, gagg_ref,
    cbt, gpre, wnt, gagg, rows, cbt_sems, sems, out_sems,
):
    chunks = cbt_sems.shape[0]
    peers, slots, width = rows.shape
    nodes = gpre.shape[0]
    per, depth = peers // chunks, cbt.shape[0] // chunks
    copy = pltpu.make_async_copy
    get_w = copy(wnt_ref, wnt, sems.at[0])
    get_gpre = copy(gpre_ref.at[0], gpre, sems.at[1])
    get_cbt = [
        copy(cbt_ref.at[pl.ds(c * depth, depth)], cbt.at[pl.ds(c * depth, depth)], cbt_sems.at[c])
        for c in range(chunks)
    ]
    loads = Stream([get_w, get_gpre] + get_cbt, 3)
    outs = []

    def put(src, dst):
        outs.append(copy(src, dst, out_sems.at[len(outs)]))
        outs[-1].start()

    loads.wait(get_w, get_gpre)
    gagg[...] = dot(gpre[...], wnt[...]).astype(BF16)
    put(gagg, gagg_ref)
    for c in range(chunks):
        loads.wait(get_cbt[c])
        got = dot(cbt[c * depth : (c + 1) * depth, :], gagg[...]).astype(BF16)
        at = pl.ds(c * per, per)
        rows[at] = got.reshape(per, slots, width)
        put(rows.at[at], out_ref.at[at, :, pl.ds(0, width)])
    for c in outs:
        c.wait()


def boundary(cbt, grad_pre, w_neigh_t, peers, slots):
    bnd, nodes = cbt.shape
    width = grad_pre.shape[2]
    chunks = 4
    vmem = pltpu.VMEM
    return pl.pallas_call(
        boundary_kernel,
        out_shape=[
            jax.ShapeDtypeStruct((peers, slots, width + LANES), BF16),
            jax.ShapeDtypeStruct((nodes, width), BF16),
        ],
        in_specs=[anywhere()] * 3,
        out_specs=[anywhere()] * 2,
        scratch_shapes=[
            vmem((bnd, nodes), BF16),
            vmem((nodes, width), BF16),
            vmem((width, width), BF16),
            vmem((nodes, width), BF16),
            vmem((peers, slots, width), BF16),
            pltpu.SemaphoreType.DMA((chunks,)),
            pltpu.SemaphoreType.DMA((2,)),
            pltpu.SemaphoreType.DMA((chunks + 1,)),
        ],
        compiler_params=BACK_PARAMS,
        cost_estimate=cost((bnd + width) * nodes * width, 9 * MIB),
        name="boundary_grads",
    )(cbt, grad_pre, w_neigh_t)


def feats_grad_kernel(cot_ref, gagg_ref, gpre_ref, wst_ref, stale_ref, out_ref):
    total = dot(gpre_ref[0], wst_ref[...]) + dot(cot_ref[...], gagg_ref[...])
    out_ref[...] = (total + stale_ref[...].astype(F32)).astype(BF16)


def feats_grad(cot, grad_agg, grad_pre, w_self_t, stale_bgrad):
    nodes, width = grad_agg.shape
    block = 512
    by_block = lambda w: pl.BlockSpec((block, w), lambda i: (i, 0))
    return pl.pallas_call(
        feats_grad_kernel,
        grid=(nodes // block,),
        out_shape=jax.ShapeDtypeStruct((nodes, width), BF16),
        in_specs=[
            by_block(nodes),
            whole((nodes, width)),
            pl.BlockSpec((1, block, width), lambda i: (0, i, 0)),
            whole((width, width)),
            by_block(width),
        ],
        out_specs=by_block(width),
        compiler_params=PARAMS,
        cost_estimate=cost(nodes * width * (nodes + width), 7 * MIB),
        name="feats_grad",
    )(cot, grad_agg, grad_pre, w_self_t, stale_bgrad)


def add_kernel(keep_ref, got_ref, out_ref):
    out_ref[...] = (keep_ref[...] + got_ref[...].astype(F32)).astype(BF16)


def add_pair(keep, got):
    return pl.pallas_call(
        add_kernel,
        out_shape=jax.ShapeDtypeStruct(keep.shape, BF16),
        in_specs=[in_vmem()] * 2,
        out_specs=in_vmem(),
        compiler_params=SMALL_PARAMS,
        cost_estimate=cost(keep.size, 2 * MIB),
        name="add_pair",
    )(keep, got)


def take_kernel(ret_ref, out_ref):
    out_ref[...] = ret_ref[:, :, ret_ref.shape[2] - LANES :]


def take_shares(returned):
    peers, slots, _ = returned.shape
    return pl.pallas_call(
        take_kernel,
        out_shape=jax.ShapeDtypeStruct((peers, slots, LANES), BF16),
        in_specs=[in_vmem()],
        out_specs=in_vmem(),
        compiler_params=SMALL_PARAMS,
        cost_estimate=cost(peers * slots * LANES, MIB),
        name="take_shares",
    )(returned)


def share_kernel(parts_ref, _, out_ref, buf, sem):
    total = parts_ref[0].astype(F32)
    for c in range(1, parts_ref.shape[0]):
        total += parts_ref[c].astype(F32)
    total = total.astype(BF16)
    for p in range(buf.shape[0]):
        buf[p] = total[p % 2]
    width = out_ref.shape[2] - LANES
    copy = pltpu.make_async_copy(buf, out_ref.at[:, :, pl.ds(width, LANES)], sem)
    copy.start()
    copy.wait()


def lay_shares(parts, rows):
    peers, slots, _ = rows.shape
    return pl.pallas_call(
        share_kernel,
        out_shape=jax.ShapeDtypeStruct(rows.shape, BF16),
        in_specs=[in_vmem(), anywhere()],
        out_specs=anywhere(),
        scratch_shapes=[pltpu.VMEM((peers, slots, LANES), BF16), pltpu.SemaphoreType.DMA],
        input_output_aliases={1: 0},
        compiler_params=LAY_PARAMS,
        cost_estimate=cost(parts.size, MIB),
        name="lay_shares",
    )(parts, rows)


def slots_by_lane(idx, lanes):
    slots, peers = idx.shape
    per = lanes // slots
    tall = jnp.concatenate([idx] * per, axis=0).T
    peer = lax.broadcasted_iota(jnp.int32, tall.shape, 0)
    lane = lax.broadcasted_iota(jnp.int32, tall.shape, 1)
    return jnp.where(peer % per == lane // slots, tall, 0).reshape(peers // per, per, lanes).sum(axis=1)


def scatter_kernel(idx_ref, cnt_ref, ret_ref, out_ref, *, chunks):
    peers, slots, _ = ret_ref.shape
    nodes, width = out_ref.shape
    per = peers // chunks
    idx = slots_by_lane(live_slots(idx_ref, cnt_ref), LANES)
    node_ids = lax.broadcasted_iota(jnp.int32, (nodes, LANES), 0)
    count = per * slots // LANES
    total = None
    for c in range(chunks):
        picks = [
            jnp.where(idx[n : n + 1, :] == node_ids, 1.0, 0.0).astype(BF16)
            for n in range(c * count, (c + 1) * count)
        ]
        rows = ret_ref[c * per : (c + 1) * per, :, :width].reshape(per * slots, width)
        term = dot(jnp.concatenate(picks, axis=1), rows)
        total = term if total is None else total + term
    out_ref[...] = total.astype(BF16)


def scatter(slot_rows, send_cnt, returned, nodes, chunks=4):
    width = returned.shape[2] - LANES
    return pl.pallas_call(
        functools.partial(scatter_kernel, chunks=chunks),
        out_shape=jax.ShapeDtypeStruct((nodes, width), BF16),
        in_specs=[in_vmem()] * 3,
        out_specs=in_vmem(),
        compiler_params=SMALL_PARAMS,
        cost_estimate=cost(returned.size * nodes, 4 * MIB),
        name="scatter_rows",
    )(slot_rows, send_cnt, returned)


def weights_kernel(mine_ref, other_ref, ws_ref, wn_ref):
    first = first_core()
    chips, halves, rows, lanes = mine_ref.shape
    for part, out_ref in enumerate((ws_ref, wn_ref)):
        at = pl.ds(part * (chips // 2), chips // 2)
        for h in range(halves):
            mine = mine_ref[at, h].astype(F32).reshape(chips // 2 * rows, lanes)
            other = other_ref[at, h].astype(F32).reshape(chips // 2 * rows, lanes)
            out_ref[:, h * lanes : (h + 1) * lanes] = jnp.where(first, mine, other)
            out_ref[:, (2 + h) * lanes : (3 + h) * lanes] = jnp.where(first, other, mine)


def lay_weights(mine, other, width):
    return pl.pallas_call(
        weights_kernel,
        out_shape=[jax.ShapeDtypeStruct((width, width), F32)] * 2,
        in_specs=[in_vmem()] * 2,
        out_specs=[in_vmem()] * 2,
        compiler_params=SMALL_PARAMS,
        cost_estimate=cost(width * width, 3 * MIB),
        name="lay_weights",
    )(mine, other)


def body(
    feats,
    stale_feats,
    grad_out,
    stale_bgrad,
    w_self,
    w_neigh,
    adj_tiles,
    tile_source_rows,
    tile_cnt,
    send_idx,
    send_cnt,
):
    peers, slots = send_idx.shape
    nodes, width = feats.shape
    tile_rows = adj_tiles.shape[2]
    all_tiles = (nodes + peers * slots) // tile_rows
    chips = peers // 2
    pairs = [(d, d + 1 - 2 * (d % 2)) for d in range(peers)]
    same_core = [list(range(c, peers, 2)) for c in range(2)]

    def exchange(v, groups):
        return lax.all_to_all(
            v, "dom", split_axis=0, concat_axis=0, tiled=True, axis_index_groups=groups
        )

    slot_rows = send_idx.T
    outgoing = gather(slot_rows, send_cnt, stale_feats)
    incoming = exchange(outgoing, None).reshape(peers * slots, width)
    cb, cbt, cot, self_pre, own_agg, w_self_t, w_neigh_t, late, feats_t = combine(
        tile_source_rows, tile_cnt, adj_tiles, feats, grad_out, w_self, w_neigh, all_tiles
    )
    activated, grad_pre, keep, give = layer(
        cb, incoming, self_pre, own_agg, late, feats_t, chips
    )
    got = lax.ppermute(give, "dom", pairs)
    parts = exchange(add_pair(keep, got), same_core)
    rows, grad_agg = boundary(cbt, grad_pre, w_neigh_t, peers, slots)
    returned = exchange(lay_shares(parts, rows), None)
    grad_feats = feats_grad(cot, grad_agg, grad_pre, w_self_t, stale_bgrad)
    returned, grad_feats = lax.optimization_barrier((returned, grad_feats))

    mine = take_shares(returned).reshape(keep.shape)
    other = lax.ppermute(mine, "dom", pairs)
    next_bgrad = scatter(slot_rows, send_cnt, returned, nodes)
    grad_w_self, grad_w_neigh = lay_weights(mine, other, width)
    return activated, grad_feats, next_bgrad, grad_w_self, grad_w_neigh


def solution(mesh):
    in_specs = (
        P("dom", None),
        P("dom", None),
        P("dom", None),
        P("dom", None),
        P(),
        P(),
        P("dom", None, None, None),
        P("dom", None),
        P("dom"),
        P("dom", None),
        P("dom", None),
    )
    out_specs = (P("dom", None), P("dom", None), P("dom", None), P(), P())
    return jax.shard_map(body, mesh=mesh, in_specs=in_specs, out_specs=out_specs, check_vma=False)
```
